32 devices in a mesh: tok: 8 (over z, x), col: 4 (over y, core).
Axes of the slice: x: 2, y: 2, z: 4, core: 2. Of those that a mesh axis runs over, the one named last changes fastest.
Arguments:
- layer_input: bfloat16 [16384, 1024], P('tok', 'col'), may hold values from -6 to 6
- cotangent: bfloat16 [16384, 1024], P('tok', 'col'), may hold values from -9 to 9
- doc_ids: int32 [16384], P('tok'), may hold values from 0 to 2, as said below
- positions: int32 [16384], P('tok'), may hold values from 0 to 2558, as said below
- attn_gain: float32 [1024], replicated, may hold values from 0.1 to 1.9
- mlp_gain: float32 [1024], replicated, may hold values from 0.4 to 2.4
- query_gain: float32 [128], replicated, may hold values from 0.1 to 1.9
- key_norm_gain: float32 [128], replicated, may hold values from 0.1 to 1.9
- query_weight: float32 [2048, 1024], P('col', 'tok'), may hold values from -0.1875 to 0.1875
- key_matrix: float32 [1024, 1024], P('col', 'tok'), may hold values from -0.1875 to 0.1875
- value_matrix: float32 [1024, 1024], P('col', 'tok'), may hold values from -0.1875 to 0.1875
- output_weight: float32 [2048, 1024], P('col', 'tok'), may hold values from -1 to 1
- gate_weight: float32 [3072, 1024], P('col', 'tok'), may hold values from -0.1875 to 0.1875
- up_weight: float32 [3072, 1024], P('col', 'tok')
- down_weight: float32 [3072, 1024], P('col', 'tok')
Outputs:
- layer_output: bfloat16 [16384, 1024], P('tok', 'col')
- input_grad: float32 [16384, 1024], P('tok', 'col')
- attn_gain_grad: float32 [1024], replicated
- mlp_gain_grad: float32 [1024], replicated
- query_gain_grad: float32 [128], replicated
- key_gain_grad: float32 [128], replicated
- query_weight_grad: float32 [2048, 1024], P('col', 'tok')
- key_weight_grad: float32 [1024, 1024], P('col', 'tok')
- value_weight_grad: float32 [1024, 1024], P('col', 'tok')
- output_weight_grad: float32 [2048, 1024], P('col', 'tok')
- gate_weight_grad: float32 [3072, 1024], P('col', 'tok')
- up_weight_grad: float32 [3072, 1024], P('col', 'tok')
- down_weight_grad: float32 [3072, 1024], P('col', 'tok')
The draws below stay inside these ranges and needn't reach their ends.
Inputs may be any that keep to these rules, and one draw needn't show every extreme that they name: `doc_ids`: within each aligned block of 1024 tokens the ids number the documents from 0 upward and never fall; the tokens with one id in one block form one document, and no document crosses a block's end. `positions`: inside a document the position rises by 1 or 2 from one token to the next.
All inputs are finite; a program needn't handle non-finite values.
Results may differ from the reference program's by a relative error of at most 0.013.
Values may be sent and summed in bfloat16 or wider, within the bound.
No kernel may reach another device: no remote copies, remote signals or barrier semaphores. Data moves between devices by JAX's collectives and lax.ppermute only.
A program may use at most 256 MiB of HBM per device.

```python
import math
import jax
import jax.numpy as jnp
from jax import lax

MODEL_WIDTH = 1024
HQ = 16
KEY_VALUE_HEADS = 8
HEAD_WIDTH = 128
FF = 3072
SEQ_LEN = 1024
TOKENS = 16384


def document_layout(key):
    seq_count = TOKENS // SEQ_LEN
    top_position = 5 * SEQ_LEN // 2 - 2
    layout_key = jax.random.fold_in(key, 11)
    cut_key, step_key, offset_key = jax.random.split(layout_key, 3)
    cut_points = jax.random.randint(cut_key, (seq_count, 2), 0, SEQ_LEN + 1)
    position_index = jnp.arange(SEQ_LEN, dtype=jnp.int32)[None, :]
    lower_cut = jnp.minimum(cut_points[:, 0:1], cut_points[:, 1:2])
    upper_cut = jnp.maximum(cut_points[:, 0:1], cut_points[:, 1:2])
    documents = (position_index >= lower_cut).astype(jnp.int32) + (position_index >= upper_cut).astype(jnp.int32)
    strides = jax.random.randint(step_key, (seq_count, SEQ_LEN), 1, 3)
    running = jnp.cumsum(strides, axis=1) - strides
    last_index = jnp.where(documents == 0, lower_cut - 1, jnp.where(documents == 1, upper_cut - 1, SEQ_LEN - 1))
    last_index = jnp.clip(last_index, 0, SEQ_LEN - 1).astype(jnp.int32)
    running_end = jnp.take_along_axis(running, last_index, axis=1)
    offsets = jax.random.randint(offset_key, (seq_count, 3), 0, SEQ_LEN // 2 + 1)
    doc_shift = jnp.take_along_axis(offsets, documents, axis=1)
    seq_row = jnp.arange(seq_count, dtype=jnp.int32)[:, None]
    first_last = (seq_row == 0) & (documents == documents[0:1, SEQ_LEN - 1:SEQ_LEN])
    doc_shift = jnp.where(first_last, 0, doc_shift)
    placed = top_position - doc_shift - (running_end - running)
    return (documents.reshape(-1).astype(jnp.int32), placed.reshape(-1).astype(jnp.int32))


def draw_doc_ids(key, part):
    return document_layout(key)[0]


def draw_positions(key, part):
    return document_layout(key)[1]


def rough_field(key, shape):
    return jnp.clip(jax.random.normal(key, shape, jnp.float32), -6.0, 6.0)


def input_common(key):
    return rough_field(jax.random.fold_in(key, 21), (TOKENS, MODEL_WIDTH))


def draw_layer_input(key, part):
    return input_common(key).astype(jnp.bfloat16)


def draw_cotangent(key, part):
    fresh = rough_field(jax.random.fold_in(key, 22), (TOKENS, MODEL_WIDTH))
    return (0.8 * input_common(key) + 0.6 * fresh).astype(jnp.bfloat16)


def draw_mlp_gain(key, part):
    ramp = jnp.arange(MODEL_WIDTH, dtype=jnp.float32) / (MODEL_WIDTH - 1)
    base = jnp.exp(math.log(0.5) + ramp * math.log(4.0))
    rough = jax.random.uniform(jax.random.fold_in(key, 41), (MODEL_WIDTH,), jnp.float32, 0.85, 1.15)
    return base * rough


def up_common(key):
    return rough_field(jax.random.fold_in(key, 31), (FF, MODEL_WIDTH))


def draw_up_weight(key, part):
    return up_common(key) * MODEL_WIDTH ** (-0.5)


def draw_down_weight(key, part):
    fresh = rough_field(jax.random.fold_in(key, 32), (FF, MODEL_WIDTH))
    return (0.8 * up_common(key) + 0.6 * fresh) * FF ** (-0.5)


def levels(own_key, extent, pieces, low, top_value):
    factor_of = 1.0
    for dim, blocks in pieces:
        draws = jax.random.uniform(jax.random.fold_in(jax.random.fold_in(own_key, 6), dim), (blocks,), jnp.float32, low / len(pieces), top_value / len(pieces))
        factor_of = factor_of * jnp.repeat(jnp.exp(draws), extent[dim] // blocks).reshape((-1,) + (1,) * (len(extent) - 1 - dim))
    return factor_of


def bell_draw(rng, shape, deviation, limit, cuts=(), kind=jnp.bfloat16):
    entries = jax.random.normal(rng, shape, jnp.float32) * deviation
    if len(cuts) > 0:
        entries = levels(rng, shape, cuts, -0.22, 0.18) * entries
    return jnp.clip(entries, min=-limit, max=limit).astype(kind)


def setup_inputs(seed: int = 0) -> dict:
    splits = jax.random.split(jax.random.key(seed), 16)
    layer_input = draw_layer_input(jax.random.fold_in(splits[15], 71), 0)
    cotangent = draw_cotangent(jax.random.fold_in(splits[15], 71), 0)
    doc_ids = draw_doc_ids(jax.random.fold_in(splits[15], 71), 0)
    positions = draw_positions(jax.random.fold_in(splits[15], 71), 0)
    attn_gain = jnp.clip(1.0 + 0.18 * jax.random.normal(splits[4], (MODEL_WIDTH,), jnp.float32), 0.1, 1.9)
    mlp_gain = draw_mlp_gain(jax.random.fold_in(splits[15], 71), 0)
    query_gain = jnp.clip(1.0 + 0.18 * jax.random.normal(splits[6], (HEAD_WIDTH,), jnp.float32), 0.1, 1.9)
    key_norm_gain = jnp.clip(1.0 + 0.18 * jax.random.normal(splits[7], (HEAD_WIDTH,), jnp.float32), 0.1, 1.9)
    query_weight = bell_draw(splits[8], (HQ * HEAD_WIDTH, MODEL_WIDTH), MODEL_WIDTH ** -0.5, 0.1875, ((0, 4), (1, 8)), jnp.float32)
    key_matrix = bell_draw(splits[9], (KEY_VALUE_HEADS * HEAD_WIDTH, MODEL_WIDTH), MODEL_WIDTH ** -0.5, 0.1875, ((0, 4), (1, 8)), jnp.float32)
    value_matrix = bell_draw(splits[10], (KEY_VALUE_HEADS * HEAD_WIDTH, MODEL_WIDTH), MODEL_WIDTH ** -0.5, 0.1875, ((0, 4), (1, 8)), jnp.float32)
    output_weight = bell_draw(splits[11], (HQ * HEAD_WIDTH, MODEL_WIDTH), (HQ * HEAD_WIDTH // 64) ** -0.5, 1.0, ((0, 4), (1, 8)), jnp.float32)
    gate_weight = bell_draw(splits[12], (FF, MODEL_WIDTH), MODEL_WIDTH ** -0.5, 0.1875, ((0, 4), (1, 8)), jnp.float32)
    up_weight = draw_up_weight(jax.random.fold_in(splits[15], 71), 0)
    down_weight = draw_down_weight(jax.random.fold_in(splits[15], 71), 0)
    return {"layer_input": layer_input, "cotangent": cotangent, "doc_ids": doc_ids, "positions": positions, "attn_gain": attn_gain, "mlp_gain": mlp_gain, "query_gain": query_gain, "key_norm_gain": key_norm_gain, "query_weight": query_weight, "key_matrix": key_matrix, "value_matrix": value_matrix, "output_weight": output_weight, "gate_weight": gate_weight, "up_weight": up_weight, "down_weight": down_weight}


NORM_EPS = 1e-06
ROPE_BASE = 1000000.0
MASK_FILL = -1e+30
HIGHEST = lax.Precision.HIGHEST

@jax.custom_vjp
def lower_precision(v):
    return lax.optimization_barrier(v.astype(jnp.bfloat16)).astype(jnp.float32)

@jax.custom_vjp
def low_back(v):
    return v

def low_keep(v):
    return (lower_precision(v), None)

def low_pass(kept, grad):
    return (grad,)

def back_keep(v):
    return (v, None)

def back_low(kept, grad):
    return (lower_precision(grad),)
lower_precision.defvjp(low_keep, low_pass)
low_back.defvjp(back_keep, back_low)

def angle_tables(positions, head_size):
    half_size = head_size // 2
    frequency = jnp.exp(jnp.arange(half_size, dtype=jnp.float32) * (-2.0 * math.log(ROPE_BASE) / head_size))
    angles = positions.astype(jnp.float32)[:, None] * frequency[None, :]
    return (jnp.cos(angles), jnp.sin(angles))

def head_norm(values, gain):
    return values * lax.rsqrt(lax.optimization_barrier(jnp.mean(values * values, axis=-1, keepdims=True)) + NORM_EPS) * gain

def rotate(values, cosine_lookup, sine_lookup):
    half_size = values.shape[-1] // 2
    first_half = values[..., :half_size]
    second_half = values[..., half_size:]
    cosine_wide = cosine_lookup[:, None, :]
    sine_wide = sine_lookup[:, None, :]
    return jnp.concatenate([first_half * cosine_wide - second_half * sine_wide, second_half * cosine_wide + first_half * sine_wide], axis=-1)

def arrange_heads(projected, gain, cosine_lookup, sine_lookup):
    return rotate(head_norm(projected, gain), cosine_lookup, sine_lookup)

def attend_sequence(block):
    queries, keys, values, documents = block
    group_size = queries.shape[1] // keys.shape[1]
    keys_wide = jnp.repeat(keys, group_size, axis=1)
    values_wide = jnp.repeat(values, group_size, axis=1)
    raw_scores = jnp.einsum('qhd,phd->hqp', queries, keys_wide, precision=HIGHEST) * HEAD_WIDTH ** (-0.5)
    scores = low_back(raw_scores)
    row_index = jnp.arange(SEQ_LEN, dtype=jnp.int32)
    allowed = (documents[:, None] == documents[None, :]) & (row_index[None, :] <= row_index[:, None])
    scores = jnp.where(allowed[None], scores, MASK_FILL)
    peak_score = lax.optimization_barrier(jnp.max(scores, axis=-1, keepdims=True))
    expo_scores = jnp.exp(scores - peak_score)
    probs = lower_precision(expo_scores / lax.optimization_barrier(jnp.sum(expo_scores, axis=-1, keepdims=True)))
    return jnp.einsum('hqp,phd->qhd', probs, values_wide, precision=HIGHEST)

def forward(input_float, weights, doc_block, cosine_lookup, sine_lookup):
    attn_gain, mlp_gain, query_gain, key_norm_gain, query_weight, key_matrix, value_matrix, output_weight, gate_weight, up_weight, down_weight = weights
    count_of_rows = input_float.shape[0]
    normed_one = lower_precision(input_float * lax.rsqrt(lax.optimization_barrier(jnp.mean(input_float * input_float, axis=-1, keepdims=True)) + NORM_EPS) * attn_gain)
    query_proj = low_back(jnp.dot(normed_one, lower_precision(query_weight).T, precision=HIGHEST))
    key_projected = low_back(jnp.dot(normed_one, lower_precision(key_matrix).T, precision=HIGHEST))
    value_projected = low_back(lower_precision(jnp.dot(normed_one, lower_precision(value_matrix).T, precision=HIGHEST)))
    query_att = lower_precision(arrange_heads(query_proj.reshape(count_of_rows, HQ, HEAD_WIDTH), query_gain, cosine_lookup, sine_lookup))
    key_attention = lower_precision(arrange_heads(key_projected.reshape(count_of_rows, KEY_VALUE_HEADS, HEAD_WIDTH), key_norm_gain, cosine_lookup, sine_lookup))
    value_attention = value_projected.reshape(count_of_rows, KEY_VALUE_HEADS, HEAD_WIDTH)
    seq_count = count_of_rows // SEQ_LEN

    def per_sequence(values):
        return values.reshape((seq_count, SEQ_LEN) + values.shape[1:])
    attended = lax.map(jax.checkpoint(attend_sequence), (per_sequence(query_att), per_sequence(key_attention), per_sequence(value_attention), per_sequence(doc_block)))
    mixed = low_back(lower_precision(attended.reshape(count_of_rows, HQ * HEAD_WIDTH)))
    residual = input_float + low_back(jnp.dot(mixed, lower_precision(output_weight), precision=HIGHEST))
    normed_two = lower_precision(residual * lax.rsqrt(lax.optimization_barrier(jnp.mean(residual * residual, axis=-1, keepdims=True)) + NORM_EPS) * mlp_gain)
    gate_proj = low_back(jnp.dot(normed_two, lower_precision(gate_weight).T, precision=HIGHEST))
    up_proj = low_back(jnp.dot(normed_two, lower_precision(up_weight).T, precision=HIGHEST))
    hidden = lower_precision(jax.nn.silu(gate_proj) * up_proj)
    return residual + jnp.dot(hidden, lower_precision(down_weight), precision=HIGHEST)

def reference(layer_input, cotangent, doc_ids, positions, attn_gain, mlp_gain, query_gain, key_norm_gain, query_weight, key_matrix, value_matrix, output_weight, gate_weight, up_weight, down_weight):
    seq_count = layer_input.shape[0] // SEQ_LEN
    group_seqs = math.gcd(seq_count, 4)
    group_count = seq_count // group_seqs
    group_rows = group_seqs * SEQ_LEN
    weights = (attn_gain, mlp_gain, query_gain, key_norm_gain, query_weight, key_matrix, value_matrix, output_weight, gate_weight, up_weight, down_weight)

    def group_step(totals, block):
        input_block, cot_block, doc_block, pos_block = block
        cosine_lookup, sine_lookup = angle_tables(pos_block, HEAD_WIDTH)

        def layer(input_float, params):
            return forward(input_float, params, doc_block, cosine_lookup, sine_lookup)
        result, pull = jax.vjp(layer, input_block.astype(jnp.float32), weights)
        input_part, weight_parts = pull(cot_block.astype(jnp.float32))
        new_totals = tuple((total + part for total, part in zip(totals, weight_parts)))
        return (new_totals, (result.astype(jnp.bfloat16), input_part))
    start_totals = tuple((jnp.zeros(weight.shape, jnp.float32) for weight in weights))
    totals, (outputs, input_grads) = lax.scan(group_step, start_totals, (layer_input.reshape(group_count, group_rows, MODEL_WIDTH), cotangent.reshape(group_count, group_rows, MODEL_WIDTH), doc_ids.reshape(group_count, group_rows), positions.reshape(group_count, group_rows)))
    return (outputs.reshape(-1, MODEL_WIDTH), input_grads.reshape(-1, MODEL_WIDTH), totals[0], totals[1], totals[2], totals[3], totals[4], totals[5], totals[6], totals[7], totals[8], totals[9], totals[10])
```

```python
import math
from functools import partial

import jax
import jax.numpy as jnp
from jax import lax
from jax.experimental import pallas as pl
from jax.experimental.pallas import tpu as pltpu
from jax.sharding import PartitionSpec as P

HEAD = 128
SEQ = 1024
NORM_EPS = 1e-06
ROPE_BASE = 1000000.0
NEG = -1e30
LOG2E = 1.4426950408889634
F32 = jnp.float32
BF16 = jnp.bfloat16
MIB = 1024 * 1024


def dot_nt(a, b):
    return lax.dot_general(a, b, (((1,), (1,)), ((), ())), preferred_element_type=F32)


def dot_nn(a, b):
    return lax.dot_general(a, b, (((1,), (0,)), ((), ())), preferred_element_type=F32)


def dot_tn(a, b):
    return lax.dot_general(a, b, (((0,), (0,)), ((), ())), preferred_element_type=F32)


def call(kernel, grid, ins, outs, args, table=None, scratch=(), flops=0, vmem=40):
    in_specs = [pl.BlockSpec(block, m) for block, m in ins]
    out_specs = [pl.BlockSpec(block, m) for _, _, block, m in outs]
    shapes = [jax.ShapeDtypeStruct(shape, dtype) for shape, dtype, _, _ in outs]
    nbytes = sum(a.size * a.dtype.itemsize for a in args)
    nbytes += sum(math.prod(s.shape) * s.dtype.itemsize for s in shapes)
    spec = pltpu.PrefetchScalarGridSpec(
        num_scalar_prefetch=0 if table is None else 1,
        grid=grid,
        in_specs=in_specs,
        out_specs=out_specs,
        scratch_shapes=list(scratch),
    )
    cost = pl.CostEstimate(flops=int(flops), bytes_accessed=int(nbytes), transcendentals=0)
    run = pl.pallas_call(
        kernel,
        out_shape=shapes,
        grid_spec=spec,
        cost_estimate=cost,
        compiler_params=pltpu.CompilerParams(vmem_limit_bytes=vmem * MIB),
    )
    return run(*args) if table is None else run(table, *args)


def assemble_kernel(slots, tab, a_ref, b_ref, o_ref):
    for p in range(slots):
        lanes = pl.ds(pl.multiple_of(tab[3 * p + 1] * 128, 128), 128)
        here = pl.ds(p * 128, 128)

        @pl.when(tab[3 * p + 2] == 0)
        def _():
            o_ref[:, here] = a_ref[tab[3 * p], :, lanes]

        @pl.when(tab[3 * p + 2] != 0)
        def _():
            o_ref[:, here] = b_ref[tab[3 * p], :, lanes]


def assemble_norm_kernel(slots, tab, a_ref, b_ref, gain_ref, x_ref, n_ref):
    assemble_kernel(slots, tab, a_ref, b_ref, x_ref)
    x = x_ref[...].astype(F32)
    r = lax.rsqrt(jnp.mean(x * x, axis=-1, keepdims=True) + NORM_EPS)
    n_ref[...] = (x * r * gain_ref[...]).astype(BF16)


def rope(u, cos, sin):
    return u * cos + pltpu.roll(u, HEAD // 2, axis=1) * sin


def rope_back(d, cos, sin):
    return d * cos - pltpu.roll(d, HEAD // 2, axis=1) * sin


def project_kernel(groups, n_ref, w_ref, cos_ref, sin_ref, qg_ref, kg_ref, o_ref, u_ref, r_ref):
    n = n_ref[...]
    cos, sin = cos_ref[...], sin_ref[...]
    lane = lax.broadcasted_iota(jnp.int32, (n.shape[0], 128), 1)
    inverses = jnp.zeros((n.shape[0], 128), F32)
    for g in range(groups):
        out = dot_nt(n, w_ref[pl.ds(g * 512, 512), :])
        for i in range(3):
            u = out[:, i * 128 : (i + 1) * 128]
            r = lax.rsqrt(jnp.mean(u * u, axis=-1, keepdims=True) + NORM_EPS)
            u = u * r
            gain = qg_ref[...] if i < 2 else kg_ref[...]
            o_ref[:, pl.ds(g * 512 + i * 128, 128)] = rope(u * gain, cos, sin).astype(BF16)
            u_ref[:, pl.ds(g * 384 + i * 128, 128)] = u.astype(BF16)
            inverses = jnp.where(lane == g * 3 + i, r, inverses)
        o_ref[:, pl.ds(g * 512 + 384, 128)] = out[:, 384:].astype(BF16)
    r_ref[...] = inverses


def visible(start_ref, first, rows, last):
    start = start_ref[:, pl.ds(first, rows)]
    start = jnp.concatenate([start, start], axis=1)
    key = lax.broadcasted_iota(jnp.int32, (last, 2 * rows), 0)
    query = lax.broadcasted_iota(jnp.int32, (1, 2 * rows), 1)
    query = jnp.where(query >= rows, query - rows, query) + first
    return (key >= start) & (key <= query)


def attend_kernel(rows, qkv_ref, start_ref, o_ref, l_ref):
    scale = HEAD**-0.5 * LOG2E
    for i in range(SEQ // rows):
        first, last = i * rows, (i + 1) * rows
        span = pl.ds(first, rows)
        q = jnp.concatenate([qkv_ref[span, 0:128], qkv_ref[span, 128:256]], axis=0)
        s = dot_nt(qkv_ref[0:last, 256:384], q) * scale
        s = jnp.where(visible(start_ref, first, rows, last), s, NEG)
        m = jnp.max(s, axis=0, keepdims=True)
        e = jnp.exp2(s - m)
        total = jnp.sum(e, axis=0, keepdims=True)
        o = dot_tn(qkv_ref[0:last, 384:512], e.astype(BF16)) * (1.0 / total)
        o = o.T.astype(BF16)
        o_ref[span, 0:128] = o[:rows]
        o_ref[span, 128:256] = o[rows:]
        log_total = m + jnp.log2(total)
        l_ref[0, 0:1, span] = log_total[:, :rows]
        l_ref[0, 1:2, span] = log_total[:, rows:]


def attend_back_kernel(
    rows, qkv_ref, do_ref, l_ref, start_ref, u_ref, r_ref, cos_ref, sin_ref, qg_ref, kg_ref,
    o_ref, gain_ref, dk_ref, dv_ref,
):
    g = pl.program_id(0)
    scale = HEAD**-0.5

    @pl.when(g == 0)
    def _():
        gain_ref[...] = jnp.zeros_like(gain_ref)

    lane = lax.broadcasted_iota(jnp.int32, (SEQ, 128), 1)

    def through(grad, head, span, gain):
        u = u_ref[span, pl.ds(head * 128, 128)].astype(F32)
        picked = jnp.where(lane[: grad.shape[0]] == g * 3 + head, r_ref[span, :], 0.0)
        r = jnp.sum(picked, axis=-1, keepdims=True)
        d = rope_back(grad, cos_ref[span, :], sin_ref[span, :])
        gain_part = jnp.sum(d * u, axis=0, keepdims=True)
        d = d * gain
        d = r * (d - u * jnp.mean(u * d, axis=-1, keepdims=True))
        return d.astype(BF16), gain_part

    q_part = jnp.zeros((1, HEAD), F32)
    for i in reversed(range(SEQ // rows)):
        first, last = i * rows, (i + 1) * rows
        span = pl.ds(first, rows)
        keys = pl.ds(0, last)
        q = jnp.concatenate([qkv_ref[span, 0:128], qkv_ref[span, 128:256]], axis=0)
        do = jnp.concatenate([do_ref[span, 0:128], do_ref[span, 128:256]], axis=0)
        log_total = jnp.concatenate([l_ref[0, 0:1, span], l_ref[0, 1:2, span]], axis=1)
        k = qkv_ref[0:last, 256:384]
        s = dot_nt(k, q) * (scale * LOG2E)
        s = jnp.where(visible(start_ref, first, rows, last), s, NEG)
        p = jnp.exp2(s - log_total)
        t = p * dot_nt(qkv_ref[0:last, 384:512], do)
        ds = (t - p * jnp.sum(t, axis=0, keepdims=True)).astype(BF16)
        dv = dot_nn(p.astype(BF16), do)
        dk = dot_nn(ds, q)
        if last == SEQ:
            dv_ref[...] = dv
            dk_ref[...] = dk
        else:
            dv_ref[keys, :] += dv
            dk_ref[keys, :] += dk
        dq = (dot_tn(k, ds) * scale).T
        for head in range(2):
            out, part = through(dq[head * rows : (head + 1) * rows], head, span, qg_ref[...])
            o_ref[span, pl.ds(head * 128, 128)] = out
            q_part += part
    out, k_part = through(dk_ref[...] * scale, 2, pl.ds(0, SEQ), kg_ref[...])
    o_ref[:, 256:384] = out
    o_ref[:, 384:512] = dv_ref[...].astype(BF16)
    gain_ref[0:1, :] += q_part
    gain_ref[1:2, :] += k_part


def residual_kernel(parts, x_ref, *refs):
    total = x_ref[...].astype(F32)
    for ref in refs[:parts]:
        total += ref[...].astype(F32)
    gain_ref, res_ref, n_ref = refs[parts:]
    r = lax.rsqrt(jnp.mean(total * total, axis=-1, keepdims=True) + NORM_EPS)
    res_ref[...] = total
    n_ref[...] = (total * r * gain_ref[...]).astype(BF16)


def ffn_kernel(n_ref, c_ref, wg_ref, wu_ref, wd_ref, h_ref, dg_ref, du_ref, f_ref, t_ref):
    n = n_ref[...]
    gate = dot_nt(n, wg_ref[...])
    up = dot_nt(n, wu_ref[...])
    dh = dot_nt(c_ref[...], wd_ref[...])
    sig = 1.0 / (1.0 + jnp.exp2(gate * -LOG2E))
    act = gate * sig
    hidden = (act * up).astype(BF16)
    du = (dh * act).astype(BF16)
    dg = (dh * up * sig * (1.0 + gate * (1.0 - sig))).astype(BF16)
    h_ref[...] = hidden
    dg_ref[...] = dg
    du_ref[...] = du
    f_ref[...] = dot_nn(hidden, wd_ref[...]).astype(BF16)
    t_ref[...] = (dot_nn(dg, wg_ref[...]) + dot_nn(du, wu_ref[...])).astype(BF16)


def sum_parts(whole, halves, tab):
    total = None
    for ref in whole:
        part = ref[...].astype(F32)
        total = part if total is None else total + part
    if halves:
        per = pl.num_programs(0) // 2
        mine = pl.program_id(0) // per == tab[0]
        total += jnp.where(mine, halves[0][...].astype(F32), halves[1][...].astype(F32))
    return total


def pick_blocks(count, tab, base, source, own_ref, send_ref):
    for which, ref in enumerate((own_ref, send_ref)):
        for i in range(count):
            at = tab[base + which * count + i]
            lanes = pl.ds(pl.multiple_of(at * 128, 128), 128)
            ref[:, i * 128 : (i + 1) * 128] = source[:, lanes].astype(ref.dtype)


def middle_kernel(whole, half, tab, res_ref, cot_ref, gain_ref, *refs):
    two = sum_parts(refs[:whole], refs[whole : whole + half], tab)
    dres_ref, low_ref, part_ref = refs[whole + half :]
    res = res_ref[...]
    width = res.shape[-1]
    r = lax.rsqrt(jnp.mean(res * res, axis=-1, keepdims=True) + NORM_EPS)
    scaled = two * gain_ref[...]
    inner = jnp.sum(scaled * res, axis=-1, keepdims=True)
    grad = cot_ref[...].astype(F32) + r * scaled - res * (r * r * r * (inner / width))
    dres_ref[...] = grad
    low_ref[...] = grad.astype(BF16)

    @pl.when(pl.program_id(0) == 0)
    def _():
        part_ref[...] = jnp.zeros_like(part_ref)

    part_ref[...] += jnp.sum(two * res * r, axis=0, keepdims=True)


def output_kernel(whole, half, count, tab, res_ref, *refs):
    total = sum_parts(refs[:whole], refs[whole : whole + half], tab)
    own_ref, send_ref, hold = refs[whole + half :]
    hold[...] = res_ref[...] + total
    pick_blocks(count, tab, 1, hold, own_ref, send_ref)


def final_kernel(whole, half, count, tab, x_ref, dres_ref, gain_ref, *refs):
    one = sum_parts(refs[:whole], refs[whole : whole + half], tab)
    own_ref, send_ref, part_ref, hold = refs[whole + half :]
    x = x_ref[...].astype(F32)
    width = x.shape[-1]
    r = lax.rsqrt(jnp.mean(x * x, axis=-1, keepdims=True) + NORM_EPS)
    scaled = one * gain_ref[...]
    inner = jnp.sum(scaled * x, axis=-1, keepdims=True)
    hold[...] = dres_ref[...] + r * scaled - x * (r * r * r * (inner / width))
    pick_blocks(count, tab, 1, hold, own_ref, send_ref)

    @pl.when(pl.program_id(0) == 0)
    def _():
        part_ref[...] = jnp.zeros_like(part_ref)

    part_ref[...] += jnp.sum(one * x * r, axis=0, keepdims=True)


def grad_kernel(pairs, *refs):
    total = None
    for i in range(pairs):
        part = dot_tn(refs[2 * i][...], refs[2 * i + 1][...])
        total = part if total is None else total + part
    lo_ref, hi_ref = refs[2 * pairs :]
    half = lo_ref.shape[-1]
    lo_ref[...] = total[:, :half].astype(BF16)
    hi_ref[...] = total[:, half:].astype(BF16)


def weight_grad(pairs, first, count, block=256):
    rows, width = pairs[0][1].shape
    block = min(block, count)
    base = first // block
    ins, args = [], []
    for a, b in pairs:
        ins += [((rows, block), lambda i: (0, base + i)), ((rows, width), lambda i: (0, 0))]
        args += [a, b]
    out = ((count, width // 2), BF16, (block, width // 2), lambda i: (i, 0))
    return call(
        partial(grad_kernel, len(pairs)),
        (count // block,),
        ins,
        [out, out],
        args,
        flops=2 * rows * count * width * len(pairs),
    )


def ffn(n, cot, cot_first, w_gate, w_up, w_down, block=256):
    rows, width = n.shape
    hidden = w_gate.shape[0]
    base = cot_first // block
    row = ((block, width), lambda i: (i, 0))
    weight = ((hidden, width), lambda i: (0, 0))
    inner = ((rows, hidden), BF16, (block, hidden), lambda i: (i, 0))
    outer = ((rows, width), BF16, (block, width), lambda i: (i, 0))
    return call(
        ffn_kernel,
        (rows // block,),
        [row, ((block, width), lambda i: (base + i, 0)), weight, weight, weight],
        [inner, inner, inner, outer, outer],
        [n, cot, w_gate, w_up, w_down],
        flops=12 * rows * width * hidden,
        vmem=48,
    )


def row_specs(parts, halves, block, width, rows):
    per = rows // block // 2
    ins = [((block, width), lambda i, *_: (i, 0)) for _ in parts]
    ins += [((block, width), lambda i, *_: (i % per, 0)) for _ in halves]
    return ins


def local(
    layer_input, cotangent, doc_ids, positions, attn_gain, mlp_gain, query_gain, key_norm_gain,
    query_weight, key_matrix, value_matrix, output_weight, gate_weight, up_weight, down_weight,
):
    rows, lane_width = layer_input.shape
    nt, nc = lax.axis_size("tok"), lax.axis_size("col")
    width = lane_width * nc
    half = nc // 2
    tok, col = lax.axis_index("tok"), lax.axis_index("col")
    dp, tp = col // half, col % half
    fast = nt == 8 and nc == 4 and width // nt == 128
    chunks = lane_width // 128

    def swap_dp(a):
        return lax.ppermute(a, "col", [(j, (j + half) % nc) for j in range(nc)])

    def swap_core(a):
        return lax.ppermute(a, "col", [(j, j ^ 1) for j in range(nc)])

    groups = [[d * half + t for t in range(half)] for d in range(2)]

    def sum_tp(a):
        return lax.psum(a.astype(F32), "col", axis_index_groups=groups)

    def swap_x(a):
        return lax.ppermute(a, "tok", [(t, t ^ 1) for t in range(nt)])

    def from_z(a, k):
        return lax.ppermute(a, "tok", [(t, ((t // 2 - k) % 4) * 2 + t % 2) for t in range(nt)])

    def to_z(a, k):
        return lax.ppermute(a, "tok", [(t, ((t // 2 + k) % 4) * 2 + t % 2) for t in range(nt)])

    if fast:
        z, x = tok // 2, tok % 2
        order = [((z + p % 4) % 4) * 2 + (x ^ (p // 4)) for p in range(8)]

        def slot_of(t):
            return ((t % 2) ^ x) * 4 + (t // 2 - z) % 4

        pieces = nt
    else:
        pieces = width // 128
        order = list(range(pieces))

        def slot_of(t):
            return t

    def arrange(v):
        parts = [lax.dynamic_slice(v, (128 * t,), (128,)) for t in order]
        return jnp.concatenate(parts)[None, :]

    def restore(v):
        return jnp.concatenate(
            [lax.dynamic_slice(v, (128 * slot_of(t),), (128,)) for t in range(pieces)]
        )

    out_table = [tp]
    for block in (col, (col + half) % nc):
        out_table += [slot_of(block * chunks + i) for i in range(chunks)]
    out_table = jnp.stack([jnp.asarray(t, jnp.int32) for t in out_table])

    kv_rows = key_matrix.shape[0] // HEAD
    mixed_weight = []
    for g in range(kv_rows):
        mixed_weight += [
            query_weight[g * 256 : (g + 1) * 256],
            key_matrix[g * 128 : (g + 1) * 128],
            value_matrix[g * 128 : (g + 1) * 128],
        ]
    own_qkv = jnp.concatenate(mixed_weight, axis=0).astype(BF16)
    own_out = output_weight.astype(BF16)
    own_up = jnp.concatenate([gate_weight, up_weight], axis=0).astype(BF16)
    own_down = down_weight.astype(BF16)
    hidden = gate_weight.shape[0]

    if fast:

        def gather_z(p):
            return [p] + [from_z(p, k) for k in (1, 2, 3)]

        def gather(p):
            return jnp.concatenate((own := gather_z(p)) + [swap_x(q) for q in own], axis=1)

        def gather_x_last(p):
            own = gather_z(p)
            other = [swap_dp(q) for q in own]
            own, other = own + [swap_x(q) for q in own], other + [swap_x(q) for q in other]
            return jnp.concatenate(
                [jnp.concatenate(own, axis=1), jnp.concatenate(other, axis=1)], axis=0
            )

        def gather_y_last(p):
            own = gather_z(p)
            own = own + [swap_x(q) for q in own]
            other = [swap_dp(q) for q in own]
            return jnp.concatenate(
                [jnp.concatenate(own, axis=1), jnp.concatenate(other, axis=1)], axis=0
            )

    else:

        def gather(p):
            return lax.all_gather(p, "tok", axis=1, tiled=True)

        def gather_x_last(p):
            own = gather(p)
            return jnp.concatenate([own, swap_dp(own)], axis=0)

        gather_y_last = gather_x_last

    gain_one, gain_two = arrange(attn_gain), arrange(mlp_gain)

    def seq_rows(a, which):
        return lax.dynamic_slice_in_dim(a, which * SEQ, SEQ, axis=0)

    if fast:
        in_table = []
        for t in order:
            block = t // chunks
            in_table += [
                (block // half != dp).astype(jnp.int32),
                t % chunks,
                (block % half != tp).astype(jnp.int32),
            ]
        in_table = jnp.stack(in_table)
        got = swap_dp(seq_rows(layer_input, 1 - dp))
        mine = jnp.stack([seq_rows(layer_input, dp), got])
        other = swap_core(mine)
        spec = ((2, 256, lane_width), lambda i, *_: (0, i, 0))
        row = ((SEQ, width), BF16, (256, width), lambda i, *_: (i, 0))
        x_rows, normed_one = call(
            partial(assemble_norm_kernel, pieces),
            (SEQ // 256,),
            [spec, spec, ((1, width), lambda i, *_: (0, 0))],
            [row, row],
            [mine, other, gain_one],
            table=in_table,
        )
        cot_mine = jnp.stack([cotangent, swap_dp(cotangent)])
        cot_other = swap_core(cot_mine)

        def cot_map(i, tab):
            d, t = tab[24], tab[25]
            return (0, jnp.where(i < 2, d * 2 + i, (1 - d) * 2 + (i - 2 + t) % 2), 0)

        spec = ((2, 512, lane_width), cot_map)
        cot_rows = call(
            partial(assemble_kernel, pieces),
            (4,),
            [spec, spec],
            [((2 * SEQ, width), BF16, (512, width), lambda i, *_: (i, 0))],
            [cot_mine, cot_other],
            table=jnp.concatenate([in_table, jnp.stack([dp, tp]).astype(jnp.int32)]),
        )[0]
    else:
        whole_input = lax.all_gather(layer_input, "col", axis=1, tiled=True)
        whole_cot = lax.all_gather(cotangent, "col", axis=1, tiled=True)
        x_rows = seq_rows(whole_input, dp)
        cot_rows = jnp.concatenate([seq_rows(whole_cot, dp), seq_rows(whole_cot, 1 - dp)], axis=0)
        wide = x_rows.astype(F32)
        inverse = lax.rsqrt(jnp.mean(wide * wide, axis=-1, keepdims=True) + NORM_EPS)
        normed_one = (wide * inverse * gain_one).astype(BF16)

    place = lax.dynamic_slice_in_dim(positions, dp * SEQ, SEQ).astype(F32)
    steps = jnp.arange(HEAD // 2, dtype=F32)
    frequency = jnp.exp(steps * (-2.0 * math.log(ROPE_BASE) / HEAD))
    angle = place[:, None] * frequency[None, :]
    cosine, sine = jnp.cos(angle), jnp.sin(angle)
    cosine = jnp.concatenate([cosine, cosine], axis=1)
    sine = jnp.concatenate([-sine, sine], axis=1)
    docs = lax.dynamic_slice_in_dim(doc_ids, dp * SEQ, SEQ)
    start = jnp.sum((docs[:, None] < docs[None, :]).astype(jnp.int32), axis=0)[None, :]
    query_row, key_row = query_gain[None, :], key_norm_gain[None, :]

    w_qkv = gather_x_last(own_qkv)
    count = w_qkv.shape[0] // 512
    row = lambda i, *_: (i, 0)
    fixed = lambda i, *_: (0, 0)
    by_head = lambda i, *_: (0, i)
    qkv, unit, inverses = call(
        partial(project_kernel, count),
        (SEQ // 256,),
        [
            ((256, width), row),
            ((count * 512, width), fixed),
            ((256, 128), row),
            ((256, 128), row),
            ((1, 128), fixed),
            ((1, 128), fixed),
        ],
        [
            ((SEQ, count * 512), BF16, (256, count * 512), row),
            ((SEQ, count * 384), BF16, (256, count * 384), row),
            ((SEQ, 128), F32, (256, 128), row),
        ],
        [normed_one, w_qkv, cosine, sine, query_row, key_row],
        flops=2 * SEQ * width * count * 512,
    )
    head_block = lambda n: ((SEQ, n), by_head)
    log_block = ((1, 2, SEQ), lambda i, *_: (i, 0, 0))
    mixed, log_total = call(
        partial(attend_kernel, 256),
        (count,),
        [head_block(512), ((1, SEQ), fixed)],
        [
            ((SEQ, count * 256), BF16, (SEQ, 256), by_head),
            ((count, 2, SEQ), F32, (1, 2, SEQ), lambda i, *_: (i, 0, 0)),
        ],
        [qkv, start],
        flops=8 * SEQ * SEQ * HEAD * count,
    )
    w_out = gather_y_last(own_out)
    out_part = dot_nn(mixed, w_out)
    if fast:
        out_part = out_part.astype(BF16)
        parts = [out_part, swap_core(out_part)]
    else:
        parts = [sum_tp(out_part)]
    residual, normed_two = call(
        partial(residual_kernel, len(parts)),
        (SEQ // 256,),
        [((256, width), row)] * (1 + len(parts)) + [((1, width), fixed)],
        [
            ((SEQ, width), F32, (256, width), row),
            ((SEQ, width), BF16, (256, width), row),
        ],
        [x_rows, *parts, gain_two],
    )

    if fast:
        piece = lax.dynamic_slice_in_dim(normed_two, tp * (SEQ // 2), SEQ // 2, axis=0)
        piece = swap_dp(piece)
        normed_other = jnp.concatenate([piece, swap_core(piece)], axis=0)
    else:
        normed_other = swap_dp(normed_two)
    w_both = gather(own_up)
    w_gate, w_up = w_both[:hidden], w_both[hidden:]
    w_down = gather(own_down)
    hid_a, gate_a, up_a, ffn_a, two_a = ffn(normed_two, cot_rows, 0, w_gate, w_up, w_down)
    hid_b, gate_b, up_b, ffn_b, two_b = ffn(normed_other, cot_rows, SEQ, w_gate, w_up, w_down)

    if fast:

        def collect(a, b):
            mid = SEQ // 2
            mine = (b[:mid].astype(F32) + swap_core(b[mid:]).astype(F32)).astype(BF16)
            got = swap_dp(mine)
            return [a, swap_core(a)], [got, swap_core(got)]
    else:

        def collect(a, b):
            return [sum_tp(a) + swap_dp(sum_tp(b))], []

    whole, halves = collect(two_a, two_b)
    d_res, d_low, mlp_part = call(
        partial(middle_kernel, len(whole), len(halves)),
        (SEQ // 256,),
        [((256, width), row), ((256, width), row), ((1, width), fixed)]
        + row_specs(whole, halves, 256, width, SEQ),
        [
            ((SEQ, width), F32, (256, width), row),
            ((SEQ, width), BF16, (256, width), row),
            ((1, width), F32, (1, width), fixed),
        ],
        [residual, cot_rows, gain_two, *whole, *halves],
        table=out_table,
    )

    whole, halves = collect(ffn_a, ffn_b)
    own_y, send_y = call(
        partial(output_kernel, len(whole), len(halves), chunks),
        (SEQ // 256,),
        [((256, width), row)] + row_specs(whole, halves, 256, width, SEQ),
        [((SEQ, lane_width), BF16, (256, lane_width), row)] * 2,
        [residual, *whole, *halves],
        table=out_table,
        scratch=[pltpu.VMEM((256, width), F32)],
    )

    def by_sequence(own, other):
        return jnp.where(
            dp == 0,
            jnp.concatenate([own, other], axis=0),
            jnp.concatenate([other, own], axis=0),
        )

    layer_output = by_sequence(own_y, swap_dp(send_y))

    cot_a, cot_b = cot_rows[:SEQ], cot_rows[SEQ:]
    grad_down = weight_grad([(hid_a, cot_a), (hid_b, cot_b)], 0, hidden)
    grad_gate = weight_grad([(gate_a, normed_two), (gate_b, normed_other)], 0, hidden)
    grad_up = weight_grad([(up_a, normed_two), (up_b, normed_other)], 0, hidden)

    d_mixed = dot_nt(d_low, w_out).astype(BF16)
    out_rows = mixed.shape[1] // 2
    grad_out_own = weight_grad([(mixed, d_low)], 0, out_rows)
    grad_out_other = weight_grad([(mixed, d_low)], out_rows, out_rows)
    d_qkv, gain_part = call(
        partial(attend_back_kernel, 256),
        (count,),
        [
            head_block(512),
            head_block(256),
            log_block,
            ((1, SEQ), fixed),
            head_block(384),
            ((SEQ, 128), fixed),
            ((SEQ, 128), fixed),
            ((SEQ, 128), fixed),
            ((1, 128), fixed),
            ((1, 128), fixed),
        ],
        [
            ((SEQ, count * 512), BF16, (SEQ, 512), by_head),
            ((8, 128), F32, (8, 128), fixed),
        ],
        [qkv, d_mixed, log_total, start, unit, inverses, cosine, sine, query_row, key_row],
        scratch=[pltpu.VMEM((SEQ, 128), F32), pltpu.VMEM((SEQ, 128), F32)],
        flops=20 * SEQ * SEQ * HEAD * count,
    )
    one_part = dot_nn(d_qkv, w_qkv)
    if fast:
        one_part = one_part.astype(BF16)
        whole = [one_part, swap_core(one_part)]
    else:
        whole = [sum_tp(one_part)]
    own_x, send_x, attn_part = call(
        partial(final_kernel, len(whole), 0, chunks),
        (SEQ // 256,),
        [((256, width), row), ((256, width), row), ((1, width), fixed)]
        + row_specs(whole, [], 256, width, SEQ),
        [
            ((SEQ, lane_width), F32, (256, lane_width), row),
            ((SEQ, lane_width), BF16, (256, lane_width), row),
            ((1, width), F32, (1, width), fixed),
        ],
        [x_rows, d_res, gain_one, *whole],
        table=out_table,
        scratch=[pltpu.VMEM((256, width), F32)],
    )
    input_grad = by_sequence(own_x, swap_dp(send_x).astype(F32))
    qkv_rows = d_qkv.shape[1] // 2
    grad_qkv_own = weight_grad([(d_qkv, normed_one)], 0, qkv_rows)
    grad_qkv_other = weight_grad([(d_qkv, normed_one)], qkv_rows, qkv_rows)

    if fast:

        def add(a, b):
            return a.astype(F32) + b.astype(F32)

        def low_add(a, b):
            return add(a, b).astype(BF16)

        def sum_z(a):
            return a[:, :128].astype(F32) + sum(
                to_z(a[:, 128 * k : 128 * (k + 1)], k).astype(F32) for k in (1, 2, 3)
            )

        def scatter(g):
            lo, hi = g
            return sum_z(low_add(lo, swap_x(hi)))

        def scatter_x_first(own, other):
            own = low_add(own[0], swap_x(own[1]))
            other = low_add(other[0], swap_x(other[1]))
            return sum_z(low_add(own, swap_dp(other)))

        def scatter_y_first(own, other):
            lo = low_add(own[0], swap_dp(other[0]))
            hi = low_add(own[1], swap_dp(other[1]))
            return sum_z(low_add(lo, swap_x(hi)))

    else:

        def scatter(g):
            wide_grad = jnp.concatenate(g, axis=1).astype(F32)
            return lax.psum_scatter(wide_grad, "tok", scatter_dimension=1, tiled=True)

        def scatter_x_first(own, other):
            own = jnp.concatenate(own, axis=1).astype(F32)
            own += swap_dp(jnp.concatenate(other, axis=1)).astype(F32)
            return lax.psum_scatter(own, "tok", scatter_dimension=1, tiled=True)

        scatter_y_first = scatter_x_first

    sum_down, sum_gate, sum_up = scatter(grad_down), scatter(grad_gate), scatter(grad_up)
    sum_out = scatter_y_first(grad_out_own, grad_out_other)
    sum_qkv = scatter_x_first(grad_qkv_own, grad_qkv_other)
    sum_qkv = sum_qkv.reshape(kv_rows, 512, -1)
    sum_query = sum_qkv[:, :256].reshape(kv_rows * 256, -1)
    sum_key = sum_qkv[:, 256:384].reshape(kv_rows * 128, -1)
    sum_value = sum_qkv[:, 384:].reshape(kv_rows * 128, -1)

    share = 1.0 / half
    gains = lax.psum(
        jnp.concatenate(
            [
                restore(attn_part[0]) * share,
                restore(mlp_part[0]) * share,
                gain_part[0],
                gain_part[1],
            ]
        ),
        ("tok", "col"),
    )
    return (
        layer_output,
        input_grad,
        gains[:width],
        gains[width : 2 * width],
        gains[2 * width : 2 * width + 128],
        gains[2 * width + 128 :],
        sum_query,
        sum_key,
        sum_value,
        sum_out,
        sum_gate,
        sum_up,
        sum_down,
    )


def solution(mesh):
    rows, cols, both, every = P("tok"), P("col", "tok"), P("tok", "col"), P()
    in_specs = (both, both, rows, rows, every, every, every, every) + (cols,) * 7
    out_specs = (both, both, every, every, every, every) + (cols,) * 7
    return jax.shard_map(local, mesh=mesh, in_specs=in_specs, out_specs=out_specs, check_vma=False)
```

```python
import math
from functools import partial

import jax
import jax.numpy as jnp
from jax import lax
from jax.experimental import pallas as pl
from jax.experimental.pallas import tpu as pltpu
from jax.sharding import PartitionSpec as P

HEAD = 128
SEQ = 1024
NORM_EPS = 1e-06
ROPE_BASE = 1000000.0
NEG = -1e30
LOG2E = 1.4426950408889634
F32 = jnp.float32
BF16 = jnp.bfloat16
MIB = 1024 * 1024
HINT = 0.3


def dot_nt(a, b):
    return lax.dot_general(a, b, (((1,), (1,)), ((), ())), preferred_element_type=F32)


def dot_nn(a, b):
    return lax.dot_general(a, b, (((1,), (0,)), ((), ())), preferred_element_type=F32)


def dot_tn(a, b):
    return lax.dot_general(a, b, (((0,), (0,)), ((), ())), preferred_element_type=F32)


def seq(value, *after):
    return lax.optimization_barrier((value,) + after)[0]


def call(kernel, grid, ins, outs, args, table=None, scratch=(), flops=0, vmem=40):
    in_specs = [pl.BlockSpec(block, m) for block, m in ins]
    out_specs = [pl.BlockSpec(block, m) for _, _, block, m in outs]
    shapes = [jax.ShapeDtypeStruct(shape, dtype) for shape, dtype, _, _ in outs]
    nbytes = sum(a.size * a.dtype.itemsize for a in args)
    nbytes += sum(math.prod(s.shape) * s.dtype.itemsize for s in shapes)
    spec = pltpu.PrefetchScalarGridSpec(
        num_scalar_prefetch=0 if table is None else 1,
        grid=grid,
        in_specs=in_specs,
        out_specs=out_specs,
        scratch_shapes=list(scratch),
    )
    cost = pl.CostEstimate(flops=int(flops * HINT), bytes_accessed=int(nbytes * HINT), transcendentals=0)
    run = pl.pallas_call(
        kernel,
        out_shape=shapes,
        grid_spec=spec,
        cost_estimate=cost,
        compiler_params=pltpu.CompilerParams(vmem_limit_bytes=vmem * MIB),
    )
    return run(*args) if table is None else run(table, *args)


def assemble_kernel(slots, tab, a_ref, b_ref, o_ref):
    for p in range(slots):
        lanes = pl.ds(pl.multiple_of(tab[3 * p + 1] * 128, 128), 128)
        here = pl.ds(p * 128, 128)

        @pl.when(tab[3 * p + 2] == 0)
        def _():
            o_ref[:, here] = a_ref[tab[3 * p], :, lanes]

        @pl.when(tab[3 * p + 2] != 0)
        def _():
            o_ref[:, here] = b_ref[tab[3 * p], :, lanes]


def assemble_norm_kernel(slots, tab, a_ref, b_ref, gain_ref, x_ref, n_ref):
    assemble_kernel(slots, tab, a_ref, b_ref, x_ref)
    x = x_ref[...].astype(F32)
    r = lax.rsqrt(jnp.mean(x * x, axis=-1, keepdims=True) + NORM_EPS)
    n_ref[...] = (x * r * gain_ref[...]).astype(BF16)


def rope(u, cos, sin):
    return u * cos + pltpu.roll(u, HEAD // 2, axis=1) * sin


def rope_back(d, cos, sin):
    return d * cos - pltpu.roll(d, HEAD // 2, axis=1) * sin


def place(tab, w_ref, first, own_ref, across_ref):
    rows = pl.ds(first, own_ref.shape[1])
    for t in range(2 * own_ref.shape[0]):
        cols = pl.ds(t * 128, 128)

        @pl.when(tab[0] == t % 2)
        def _():
            w_ref[rows, cols] = own_ref[t // 2]

        @pl.when(tab[0] != t % 2)
        def _():
            w_ref[rows, cols] = across_ref[t // 2]


def project_kernel(groups, stacks, tab, n_ref, cos_ref, sin_ref, qg_ref, kg_ref, *refs):
    if stacks:
        o_ref, u_ref, r_ref, w_ref = refs[stacks:]

        @pl.when(pl.program_id(0) == 0)
        def _():
            near, across, far, corner_a, corner_b = refs[:stacks]
            rows = near.shape[1]
            mid = rows // 2
            place(tab, w_ref, 0, near, across)
            place(tab, w_ref, rows, far.at[:, 0:mid], corner_a)
            place(tab, w_ref, rows + mid, far.at[:, mid:rows], corner_b)
    else:
        w_ref, o_ref, u_ref, r_ref = refs
    n = n_ref[...]
    cos, sin = cos_ref[...], sin_ref[...]
    lane = lax.broadcasted_iota(jnp.int32, (n.shape[0], 128), 1)
    inverses = jnp.zeros((n.shape[0], 128), F32)
    for g in range(groups):
        out = dot_nt(n, w_ref[pl.ds(g * 512, 512), :])
        for i in range(3):
            u = out[:, i * 128 : (i + 1) * 128]
            r = lax.rsqrt(jnp.mean(u * u, axis=-1, keepdims=True) + NORM_EPS)
            u = u * r
            gain = qg_ref[...] if i < 2 else kg_ref[...]
            o_ref[:, pl.ds(g * 512 + i * 128, 128)] = rope(u * gain, cos, sin).astype(BF16)
            u_ref[:, pl.ds(g * 384 + i * 128, 128)] = u.astype(BF16)
            inverses = jnp.where(lane == g * 3 + i, r, inverses)
        o_ref[:, pl.ds(g * 512 + 384, 128)] = out[:, 384:].astype(BF16)
    r_ref[...] = inverses


def out_kernel(stacks, tab, m_ref, *refs):
    o_ref, w_ref = refs[2 * stacks :]

    @pl.when(pl.program_id(0) == 0)
    def _():
        for i in range(stacks):
            place(tab, w_ref, i * refs[2 * i].shape[1], refs[2 * i], refs[2 * i + 1])

    o_ref[...] = dot_nn(m_ref[...], w_ref[...]).astype(o_ref.dtype)


def visible(start_ref, first, rows, last):
    start = start_ref[:, pl.ds(first, rows)]
    start = jnp.concatenate([start, start], axis=1)
    key = lax.broadcasted_iota(jnp.int32, (last, 2 * rows), 0)
    query = lax.broadcasted_iota(jnp.int32, (1, 2 * rows), 1)
    query = jnp.where(query >= rows, query - rows, query) + first
    return (key >= start) & (key <= query)


def attend_kernel(rows, qkv_ref, start_ref, o_ref, l_ref):
    scale = HEAD**-0.5 * LOG2E
    for i in range(SEQ // rows):
        first, last = i * rows, (i + 1) * rows
        span = pl.ds(first, rows)
        q = jnp.concatenate([qkv_ref[span, 0:128], qkv_ref[span, 128:256]], axis=0)
        s = dot_nt(qkv_ref[0:last, 256:384], q) * scale
        s = jnp.where(visible(start_ref, first, rows, last), s, NEG)
        m = jnp.max(s, axis=0, keepdims=True)
        e = jnp.exp2(s - m)
        total = jnp.sum(e, axis=0, keepdims=True)
        o = dot_tn(qkv_ref[0:last, 384:512], e.astype(BF16)) * (1.0 / total)
        o = o.T.astype(BF16)
        o_ref[span, 0:128] = o[:rows]
        o_ref[span, 128:256] = o[rows:]
        log_total = m + jnp.log2(total)
        l_ref[0, 0:1, span] = log_total[:, :rows]
        l_ref[0, 1:2, span] = log_total[:, rows:]


def attend_back_kernel(
    rows, base, qkv_ref, do_ref, l_ref, start_ref, u_ref, r_ref, cos_ref, sin_ref, qg_ref, kg_ref,
    o_ref, gain_ref, dk_ref, dv_ref,
):
    g = pl.program_id(0) + base
    scale = HEAD**-0.5

    @pl.when(pl.program_id(0) == 0)
    def _():
        gain_ref[...] = jnp.zeros_like(gain_ref)

    lane = lax.broadcasted_iota(jnp.int32, (SEQ, 128), 1)

    def through(grad, head, span, gain):
        u = u_ref[span, pl.ds(head * 128, 128)].astype(F32)
        picked = jnp.where(lane[: grad.shape[0]] == g * 3 + head, r_ref[span, :], 0.0)
        r = jnp.sum(picked, axis=-1, keepdims=True)
        d = rope_back(grad, cos_ref[span, :], sin_ref[span, :])
        gain_part = jnp.sum(d * u, axis=0, keepdims=True)
        d = d * gain
        d = r * (d - u * jnp.mean(u * d, axis=-1, keepdims=True))
        return d.astype(BF16), gain_part

    q_part = jnp.zeros((1, HEAD), F32)
    for i in reversed(range(SEQ // rows)):
        first, last = i * rows, (i + 1) * rows
        span = pl.ds(first, rows)
        keys = pl.ds(0, last)
        q = jnp.concatenate([qkv_ref[span, 0:128], qkv_ref[span, 128:256]], axis=0)
        do = jnp.concatenate([do_ref[span, 0:128], do_ref[span, 128:256]], axis=0)
        log_total = jnp.concatenate([l_ref[0, 0:1, span], l_ref[0, 1:2, span]], axis=1)
        k = qkv_ref[0:last, 256:384]
        s = dot_nt(k, q) * (scale * LOG2E)
        s = jnp.where(visible(start_ref, first, rows, last), s, NEG)
        p = jnp.exp2(s - log_total)
        t = p * dot_nt(qkv_ref[0:last, 384:512], do)
        ds = (t - p * jnp.sum(t, axis=0, keepdims=True)).astype(BF16)
        dv = dot_nn(p.astype(BF16), do)
        dk = dot_nn(ds, q)
        if last == SEQ:
            dv_ref[...] = dv
            dk_ref[...] = dk
        else:
            dv_ref[keys, :] += dv
            dk_ref[keys, :] += dk
        dq = (dot_tn(k, ds) * scale).T
        for head in range(2):
            out, part = through(dq[head * rows : (head + 1) * rows], head, span, qg_ref[...])
            o_ref[span, pl.ds(head * 128, 128)] = out
            q_part += part
    out, k_part = through(dk_ref[...] * scale, 2, pl.ds(0, SEQ), kg_ref[...])
    o_ref[:, 256:384] = out
    o_ref[:, 384:512] = dv_ref[...].astype(BF16)
    gain_ref[0:1, :] += q_part
    gain_ref[1:2, :] += k_part


def residual_kernel(parts, x_ref, *refs):
    total = x_ref[...].astype(F32)
    for ref in refs[:parts]:
        total += ref[...].astype(F32)
    gain_ref, res_ref, n_ref = refs[parts:]
    r = lax.rsqrt(jnp.mean(total * total, axis=-1, keepdims=True) + NORM_EPS)
    res_ref[...] = total
    n_ref[...] = (total * r * gain_ref[...]).astype(BF16)


def ffn_join_kernel(tab, n_ref, c_ref, g_ref, near_ref, across_ref, h_ref, f_ref, t_ref, w_ref):
    count = w_ref.shape[0] // 3

    @pl.when(pl.program_id(0) == 0)
    def _():
        place(tab, w_ref, 0, g_ref.at[:, 0], g_ref.at[:, 1])
        place(tab, w_ref, count, near_ref, across_ref)

    parts = [w_ref.at[pl.ds(i * count, count), :] for i in range(3)]
    ffn_kernel(n_ref, c_ref, *parts, h_ref, f_ref, t_ref)


def ffn_kernel(n_ref, c_ref, wg_ref, wu_ref, wd_ref, h_ref, f_ref, t_ref):
    n = n_ref[...]
    width = wg_ref.shape[0]
    gate = dot_nt(n, wg_ref[...])
    up = dot_nt(n, wu_ref[...])
    dh = dot_nt(c_ref[...], wd_ref[...])
    sig = 1.0 / (1.0 + jnp.exp2(gate * -LOG2E))
    act = gate * sig
    hidden = (act * up).astype(BF16)
    du = (dh * act).astype(BF16)
    dg = (dh * up * sig * (1.0 + gate * (1.0 - sig))).astype(BF16)
    h_ref[:, 0:width] = dg
    h_ref[:, width : 2 * width] = du
    h_ref[:, 2 * width :] = hidden
    f_ref[...] = dot_nn(hidden, wd_ref[...]).astype(BF16)
    t_ref[...] = (dot_nn(dg, wg_ref[...]) + dot_nn(du, wu_ref[...])).astype(BF16)


def sum_parts(whole, halves, tab):
    total = None
    for ref in whole:
        part = ref[...].astype(F32)
        total = part if total is None else total + part
    if halves:
        per = pl.num_programs(0) // 2
        mine = pl.program_id(0) // per != tab[0]
        total += jnp.where(mine, halves[0][...].astype(F32), halves[1][...].astype(F32))
    return total


def pick_blocks(count, tab, base, source, own_ref, send_ref):
    for which, ref in enumerate((own_ref, send_ref)):
        for i in range(count):
            at = tab[base + which * count + i]
            lanes = pl.ds(pl.multiple_of(at * 128, 128), 128)
            ref[:, i * 128 : (i + 1) * 128] = source[:, lanes].astype(ref.dtype)


def middle_kernel(whole, half, tab, res_ref, cot_ref, gain_ref, *refs):
    two = sum_parts(refs[:whole], refs[whole : whole + half], tab)
    dres_ref, low_ref, part_ref = refs[whole + half :]
    res = res_ref[...]
    width = res.shape[-1]
    r = lax.rsqrt(jnp.mean(res * res, axis=-1, keepdims=True) + NORM_EPS)
    scaled = two * gain_ref[...]
    inner = jnp.sum(scaled * res, axis=-1, keepdims=True)
    grad = cot_ref[...].astype(F32) + r * scaled - res * (r * r * r * (inner / width))
    dres_ref[...] = grad
    low_ref[...] = grad.astype(BF16)

    @pl.when(pl.program_id(0) == 0)
    def _():
        part_ref[...] = jnp.zeros_like(part_ref)

    part_ref[...] += jnp.sum(two * res * r, axis=0, keepdims=True)


def output_kernel(whole, half, count, tab, res_ref, *refs):
    total = sum_parts(refs[:whole], refs[whole : whole + half], tab)
    own_ref, send_ref, hold = refs[whole + half :]
    hold[...] = res_ref[...] + total
    pick_blocks(count, tab, 1, hold, own_ref, send_ref)


def final_kernel(whole, half, count, tab, x_ref, dres_ref, gain_ref, *refs):
    one = sum_parts(refs[:whole], refs[whole : whole + half], tab)
    own_ref, send_ref, part_ref, hold = refs[whole + half :]
    x = x_ref[...].astype(F32)
    width = x.shape[-1]
    r = lax.rsqrt(jnp.mean(x * x, axis=-1, keepdims=True) + NORM_EPS)
    scaled = one * gain_ref[...]
    inner = jnp.sum(scaled * x, axis=-1, keepdims=True)
    hold[...] = dres_ref[...] + r * scaled - x * (r * r * r * (inner / width))
    pick_blocks(count, tab, 1, hold, own_ref, send_ref)

    @pl.when(pl.program_id(0) == 0)
    def _():
        part_ref[...] = jnp.zeros_like(part_ref)

    part_ref[...] += jnp.sum(one * x * r, axis=0, keepdims=True)


def two_dots_kernel(a_ref, b_ref, v_ref, w_ref, o_ref):
    o_ref[...] = (dot_nn(a_ref[...], v_ref[...]) + dot_nn(b_ref[...], w_ref[...])).astype(o_ref.dtype)


def grad_kernel(tab, a_ref, b_ref, lo_ref, hi_ref):
    total = dot_tn(a_ref[...], b_ref[...]).astype(BF16)
    for t in range(2 * lo_ref.shape[0]):
        part = total[:, t * 128 : (t + 1) * 128]

        @pl.when(tab[0] == t % 2)
        def _():
            lo_ref[t // 2] = part

        @pl.when(tab[0] != t % 2)
        def _():
            hi_ref[t // 2] = part


def ffn_grad_kernel(spans, switch, *refs):
    rows, (cot_ref, o_ref) = refs[: 2 * spans], refs[2 * spans :]

    def put(total):
        total = total.astype(BF16)
        for t in range(o_ref.shape[0]):
            o_ref[t] = total[:, t * 128 : (t + 1) * 128]

    @pl.when(pl.program_id(0) < switch)
    def _():
        put(sum(dot_tn(rows[2 * i][...], rows[2 * i + 1][...]) for i in range(spans)))

    @pl.when(pl.program_id(0) >= switch)
    def _():
        first, total = 0, None
        for i in range(spans):
            count = rows[2 * i].shape[0]
            part = dot_tn(rows[2 * i][...], cot_ref[first : first + count, :])
            total = part if total is None else total + part
            first += count
        put(total)


def weight_grad(a, b, first, count, side, block=256):
    rows, width = b.shape
    block = min(block, count)
    base = first // block
    half = width // 256
    stack = ((half, count, 128), BF16, (half, block, 128), lambda i, *_: (0, i, 0))
    return call(
        grad_kernel,
        (count // block,),
        [((rows, block), lambda i, *_: (0, base + i)), ((rows, width), lambda i, *_: (0, 0))],
        [stack, stack],
        [a, b],
        table=side,
        flops=2 * rows * count * width,
    )


def ffn_grads(spans, cot, block=256):
    width = cot.shape[1]
    inner = spans[0][0].shape[1]
    block = math.gcd(block, inner // 3)
    ins, args = [], []
    for h, n in spans:
        ins += [((h.shape[0], block), lambda i: (0, i)), (n.shape, lambda i: (0, 0))]
        args += [h, n]
    pieces = width // 128
    return call(
        partial(ffn_grad_kernel, len(spans), 2 * inner // 3 // block),
        (inner // block,),
        ins + [(cot.shape, lambda i: (0, 0))],
        [((pieces, inner, 128), BF16, (pieces, block, 128), lambda i: (0, i, 0))],
        args + [cot],
        flops=2 * cot.shape[0] * inner * width,
        vmem=48,
    )[0]


def ffn(n, rows, cot, cot_first, w, side=None, block=256):
    width = n.shape[1]
    hidden = (w[0].shape[2] if side is not None else w.shape[0] // 3)
    base = cot_first // block
    outer = ((rows, width), BF16, (block, width), lambda i, *_: (i, 0))
    outs = [((rows, 3 * hidden), BF16, (block, 3 * hidden), lambda i, *_: (i, 0)), outer, outer]
    ins = [((block, width), lambda i, *_: (i, 0)), ((block, width), lambda i, *_: (base + i, 0))]
    if side is not None:
        ins += [(a.shape, lambda i, *_, k=a.ndim: (0,) * k) for a in w]
        outs += [((3 * hidden, width), BF16, (3 * hidden, width), lambda i, *_: (0, 0))]
    else:
        ins += [((hidden, width), lambda i, k=k: (k, 0)) for k in range(3)]
    return call(
        ffn_kernel if side is None else ffn_join_kernel,
        (rows // block,),
        ins,
        outs,
        [n, cot] + ([w, w, w] if side is None else w),
        table=side,
        flops=12 * rows * width * hidden,
        vmem=48,
    )


def row_specs(parts, halves, block, width, rows):
    per = rows // block // 2
    ins = [((block, width), lambda i, *_: (i, 0)) for _ in parts]
    ins += [((block, width), lambda i, *_: (i % per, 0)) for _ in halves]
    return ins


def local(
    layer_input, cotangent, doc_ids, positions, attn_gain, mlp_gain, query_gain, key_norm_gain,
    query_weight, key_matrix, value_matrix, output_weight, gate_weight, up_weight, down_weight,
):
    rows, lane_width = layer_input.shape
    nt, nc = lax.axis_size("tok"), lax.axis_size("col")
    width = lane_width * nc
    half = nc // 2
    tok, col = lax.axis_index("tok"), lax.axis_index("col")
    dp, tp = col // half, col % half
    fast = nt == 8 and nc == 4 and width // nt == 128
    chunks = lane_width // 128

    def swap_dp(a):
        return lax.ppermute(a, "col", [(j, (j + half) % nc) for j in range(nc)])

    def swap_core(a):
        return lax.ppermute(a, "col", [(j, j ^ 1) for j in range(nc)])

    groups = [[d * half + t for t in range(half)] for d in range(2)]

    def sum_tp(a):
        return lax.psum(a.astype(F32), "col", axis_index_groups=groups)

    def swap_x(a):
        return lax.ppermute(a, "tok", [(t, t ^ 1) for t in range(nt)])

    def swap_z(step, a):
        return lax.ppermute(a, "tok", [(t, (t // 2 ^ step) * 2 + t % 2) for t in range(nt)])

    lines = [[z * 2 + x for z in range(nt // 2)] for x in range(2)]

    def share_z(a):
        copies = jnp.broadcast_to(a[None], (nt // 2,) + a.shape)
        return lax.all_to_all(copies, "tok", 0, 0, axis_index_groups=lines)

    def trade_z(a):
        return lax.all_to_all(a, "tok", 0, 0, axis_index_groups=lines)

    x = tok % 2
    side = x[None].astype(jnp.int32)
    pieces = width // 128

    out_table = [tp]
    for block in (col, (col + half) % nc):
        out_table += [block * chunks + i for i in range(chunks)]
    out_table = jnp.stack([jnp.asarray(t, jnp.int32) for t in out_table])

    kv_rows = key_matrix.shape[0] // HEAD
    mixed_weight = []
    for g in range(kv_rows):
        mixed_weight += [
            query_weight[g * 256 : (g + 1) * 256],
            key_matrix[g * 128 : (g + 1) * 128],
            value_matrix[g * 128 : (g + 1) * 128],
        ]
    own_qkv = jnp.concatenate(mixed_weight, axis=0).astype(BF16)
    own_out = output_weight.astype(BF16)
    own_ffn = jnp.concatenate([gate_weight, up_weight, down_weight], axis=0).astype(BF16)
    hidden = gate_weight.shape[0]

    if not fast:

        def gather(p):
            return lax.all_gather(p, "tok", axis=1, tiled=True)

        def gather_both(p):
            own = gather(p)
            return jnp.concatenate([own, swap_dp(own)], axis=0)

    place = lax.dynamic_slice_in_dim(positions, dp * SEQ, SEQ).astype(F32)
    steps = jnp.arange(HEAD // 2, dtype=F32)
    frequency = jnp.exp(steps * (-2.0 * math.log(ROPE_BASE) / HEAD))
    angle = place[:, None] * frequency[None, :]
    cosine, sine = jnp.cos(angle), jnp.sin(angle)
    cosine = jnp.concatenate([cosine, cosine], axis=1)
    sine = jnp.concatenate([-sine, sine], axis=1)
    docs = lax.dynamic_slice_in_dim(doc_ids, dp * SEQ, SEQ)
    start = jnp.sum((docs[:, None] < docs[None, :]).astype(jnp.int32), axis=0)[None, :]
    query_row, key_row = query_gain[None, :], key_norm_gain[None, :]

    gain_one, gain_two = attn_gain[None, :], mlp_gain[None, :]

    def seq_rows(a, which):
        return lax.dynamic_slice_in_dim(a, which * SEQ, SEQ, axis=0)

    if fast:
        in_table = []
        for t in range(pieces):
            block = t // chunks
            in_table += [
                (block // half != dp).astype(jnp.int32),
                jnp.int32(t % chunks),
                (block % half != tp).astype(jnp.int32),
            ]
        in_table = jnp.stack(in_table)
        got = swap_dp(seq_rows(layer_input, 1 - dp))
        mine = jnp.stack([seq_rows(layer_input, dp), got])
        other = swap_core(mine)

        spec = ((2, 256, lane_width), lambda i, *_: (0, i, 0))
        row = ((SEQ, width), BF16, (256, width), lambda i, *_: (i, 0))
        x_rows, normed_one = call(
            partial(assemble_norm_kernel, pieces),
            (SEQ // 256,),
            [spec, spec, ((1, width), lambda i, *_: (0, 0))],
            [row, row],
            [mine, other, gain_one],
            table=in_table,
        )
        cot_near = swap_dp(seq(seq_rows(cotangent, 1 - dp), got))
        mid = own_qkv.shape[0] // 2
        qkv_z = share_z(own_qkv)
        gate_x = swap_x(own_ffn[:hidden])
        out_z = share_z(seq(own_out, qkv_z))
        qkv_x, qkv_y = swap_x(qkv_z), swap_dp(seq(qkv_z, cot_near))
        corner_x = swap_x(seq(qkv_y[:, :mid], out_z, normed_one, cosine, sine, start))
        corner_y = swap_dp(seq(qkv_x[:, mid:], out_z))
        qkv_stacks = [qkv_z, qkv_x, qkv_y, corner_x, corner_y]
        late_z = share_z(seq(own_ffn[hidden:], out_z, gate_x))
        out_z = seq(out_z, corner_x, corner_y)
        out_x, out_y = swap_x(out_z), swap_dp(out_z)
        out_xy = swap_x(out_y)
        out_stacks = [out_z, out_x, out_y, out_xy]
        gate_z = share_z(seq(jnp.stack([own_ffn[:hidden], gate_x]), late_z))
        late_x = swap_x(seq(late_z, out_xy))
        ffn_stacks = [gate_z, late_z, late_x]
        cot_far = swap_dp(seq(seq_rows(cotangent, dp), corner_y))
        cot_got = jnp.where(
            dp == 0,
            jnp.concatenate([cot_near, cot_far], axis=0),
            jnp.concatenate([cot_far, cot_near], axis=0),
        )
        cot_mine = jnp.stack([cotangent, cot_got])
        cot_other = swap_core(cot_mine)

        def cot_map(i, tab):
            d, t = tab[24], tab[25]
            return (0, jnp.where(i < 2, d * 2 + i, (1 - d) * 2 + (i - 2 + t) % 2), 0)

        spec = ((2, 512, lane_width), cot_map)
        cot_rows = call(
            partial(assemble_kernel, pieces),
            (4,),
            [spec, spec],
            [((2 * SEQ, width), BF16, (512, width), lambda i, *_: (i, 0))],
            [cot_mine, cot_other],
            table=jnp.concatenate([in_table, jnp.stack([dp, tp]).astype(jnp.int32)]),
        )[0]
    else:
        w_qkv, w_out = gather_both(own_qkv), gather_both(own_out)
        w_ffn = gather(own_ffn)
        whole_input = lax.all_gather(layer_input, "col", axis=1, tiled=True)
        whole_cot = lax.all_gather(cotangent, "col", axis=1, tiled=True)
        x_rows = seq_rows(whole_input, dp)
        cot_rows = jnp.concatenate([seq_rows(whole_cot, dp), seq_rows(whole_cot, 1 - dp)], axis=0)
        wide = x_rows.astype(F32)
        inverse = lax.rsqrt(jnp.mean(wide * wide, axis=-1, keepdims=True) + NORM_EPS)
        normed_one = (wide * inverse * gain_one).astype(BF16)

    count = 2 * kv_rows
    row = lambda i, *_: (i, 0)
    fixed = lambda i, *_: (0, 0)
    by_head = lambda i, *_: (0, i)
    stack_spec = lambda a: (a.shape, lambda i, *_: (0, 0, 0))
    ins = [
        ((256, width), row),
        ((256, 128), row),
        ((256, 128), row),
        ((1, 128), fixed),
        ((1, 128), fixed),
    ]
    outs = [
        ((SEQ, count * 512), BF16, (256, count * 512), row),
        ((SEQ, count * 384), BF16, (256, count * 384), row),
        ((SEQ, 128), F32, (256, 128), row),
    ]
    args = [normed_one, cosine, sine, query_row, key_row]
    whole_w = ((count * 512, width), fixed)
    project_flops = 2 * SEQ * width * count * 512
    if fast:
        qkv, unit, inverses, w_qkv = call(
            partial(project_kernel, count, len(qkv_stacks)),
            (SEQ // 256,),
            ins + [stack_spec(a) for a in qkv_stacks],
            outs + [((count * 512, width), BF16, *whole_w)],
            args + qkv_stacks,
            table=side,
            flops=project_flops,
        )
    else:
        qkv, unit, inverses = call(
            partial(project_kernel, count, 0),
            (SEQ // 256,),
            ins + [whole_w],
            outs,
            args + [w_qkv],
            table=side,
            flops=project_flops,
        )
    head_block = lambda n: ((SEQ, n), by_head)
    log_block = ((1, 2, SEQ), lambda i, *_: (i, 0, 0))
    mixed, log_total = call(
        partial(attend_kernel, 256),
        (count,),
        [head_block(512), ((1, SEQ), fixed)],
        [
            ((SEQ, count * 256), BF16, (SEQ, 256), by_head),
            ((count, 2, SEQ), F32, (1, 2, SEQ), lambda i, *_: (i, 0, 0)),
        ],
        [seq(qkv, out_x, out_y, late_z) if fast else qkv, start],
        flops=8 * SEQ * SEQ * HEAD * count,
    )
    if fast:
        heads_width = count * 256
        out_part, w_out = call(
            partial(out_kernel, len(out_stacks) // 2),
            (SEQ // 256,),
            [((256, heads_width), row)] + [stack_spec(a) for a in out_stacks],
            [
                ((SEQ, width), BF16, (256, width), row),
                ((heads_width, width), BF16, (heads_width, width), fixed),
            ],
            [seq(mixed, cot_far), *out_stacks],
            table=side,
            flops=2 * SEQ * heads_width * width,
        )
        parts = [out_part, swap_core(out_part)]
    else:
        parts = [sum_tp(dot_nn(mixed, w_out))]
    residual, normed_two = call(
        partial(residual_kernel, len(parts)),
        (SEQ // 256,),
        [((256, width), row)] * (1 + len(parts)) + [((1, width), fixed)],
        [
            ((SEQ, width), F32, (256, width), row),
            ((SEQ, width), BF16, (256, width), row),
        ],
        [seq(x_rows, cot_rows) if fast else x_rows, *parts, gain_two],
    )

    if fast:
        mid = SEQ // 2
        piece = lax.dynamic_slice_in_dim(normed_two, tp * mid, mid, axis=0)
        near = swap_dp(piece)
        far = swap_core(near)
        near_h, near_f, near_t, w_ffn = ffn(near, mid, cot_rows, SEQ, ffn_stacks, side)
        far_h, far_f, far_t = ffn(seq(far, near_t), mid, cot_rows, SEQ + mid, w_ffn)
        two_mine = (far_t.astype(F32) + swap_core(near_t).astype(F32)).astype(BF16)
        two_got = swap_dp(two_mine)
        own_h, own_f, own_t = ffn(seq(normed_two, two_mine), SEQ, cot_rows, 0, w_ffn)
        own_sib = swap_core(own_t)
        grad_ffn = ffn_grads([(own_h, normed_two), (near_h, near), (far_h, far)], cot_rows)
        ffn_mine = (far_f.astype(F32) + swap_core(near_f).astype(F32)).astype(BF16)
        ffn_got = swap_dp(seq(ffn_mine, two_got))
        two_sib = swap_core(seq(two_got, grad_ffn))
        grad_ffn = seq(grad_ffn, two_got)
        whole, halves = [own_t, own_sib], [two_got, two_sib]
    else:
        normed_other = swap_dp(normed_two)
        own_h, own_f, own_t = ffn(normed_two, SEQ, cot_rows, 0, w_ffn)
        other_h, other_f, other_t = ffn(normed_other, SEQ, cot_rows, SEQ, w_ffn)
        grad_ffn = ffn_grads([(own_h, normed_two), (other_h, normed_other)], cot_rows)
        whole = [sum_tp(own_t) + swap_dp(sum_tp(other_t))]
        ffn_whole = [sum_tp(own_f) + swap_dp(sum_tp(other_f))]
        halves, ffn_halves = [], []

    d_res, d_low, mlp_part = call(
        partial(middle_kernel, len(whole), len(halves)),
        (SEQ // 256,),
        [((256, width), row), ((256, width), row), ((1, width), fixed)]
        + row_specs(whole, halves, 256, width, SEQ),
        [
            ((SEQ, width), F32, (256, width), row),
            ((SEQ, width), BF16, (256, width), row),
            ((1, width), F32, (1, width), fixed),
        ],
        [residual, cot_rows, gain_two, *whole, *halves],
        table=out_table,
    )

    def by_sequence(own, other):
        return jnp.where(
            dp == 0,
            jnp.concatenate([own, other], axis=0),
            jnp.concatenate([other, own], axis=0),
        )

    def add(a, b):
        return a.astype(F32) + b.astype(F32)

    def low_add(a, b):
        return add(a, b).astype(BF16)

    d_mixed = dot_nt(d_low, w_out).astype(BF16)
    out_rows = mixed.shape[1] // 2
    grad_out_other = weight_grad(mixed, d_low, out_rows, out_rows, side)
    grad_out_own = weight_grad(mixed, d_low, 0, out_rows, side)

    def attend_back(base, some, after):
        cols = lambda n: ((SEQ, n), lambda i, *_: (0, base + i))
        return call(
            partial(attend_back_kernel, 256, base),
            (some,),
            [
                cols(512),
                cols(256),
                ((1, 2, SEQ), lambda i, *_: (base + i, 0, 0)),
                ((1, SEQ), fixed),
                cols(384),
                ((SEQ, 128), fixed),
                ((SEQ, 128), fixed),
                ((SEQ, 128), fixed),
                ((1, 128), fixed),
                ((1, 128), fixed),
            ],
            [
                ((SEQ, some * 512), BF16, (SEQ, 512), by_head),
                ((8, 128), F32, (8, 128), fixed),
            ],
            [
                qkv, seq(d_mixed, *after), log_total, start, unit, inverses, cosine, sine,
                query_row, key_row,
            ],
            scratch=[pltpu.VMEM((SEQ, 128), F32), pltpu.VMEM((SEQ, 128), F32)],
            flops=20 * SEQ * SEQ * HEAD * some,
        )

    some = count // 2
    qkv_rows = some * 512
    d_other, gains_other = attend_back(some, some, (*grad_out_other, *grad_out_own))
    grad_other = weight_grad(d_other, normed_one, 0, qkv_rows, side)
    if fast:
        out_over = swap_dp(jnp.stack(grad_out_other))
        far_lo, far_hi = grad_other
        mid = qkv_rows // 2
        corner = swap_x(far_hi[:, :mid])
        over = swap_dp(seq(jnp.stack([far_lo[:, mid:], far_hi[:, mid:]]), out_over))
    d_own, gains_own = attend_back(0, some, (*grad_other, ffn_got) if fast else grad_other)
    gain_part = gains_own + gains_other
    grad_own = weight_grad(
        seq(d_own, out_over) if fast else d_own, normed_one, 0, qkv_rows, side
    )
    if fast:
        own_lo, own_hi = grad_own
        out_lo = low_add(grad_out_own[0], out_over[0])
        out_hi = low_add(grad_out_own[1], out_over[1])
        out_across = swap_x(out_hi)
        across_a = swap_x(seq(own_hi[:, :mid], corner))
    wide = ((256, qkv_rows), row)
    one_part = call(
        two_dots_kernel,
        (SEQ // 256,),
        [
            wide,
            wide,
            ((qkv_rows, width), lambda i: (0, 0)),
            ((qkv_rows, width), lambda i: (1, 0)),
        ],
        [((SEQ, width), BF16 if fast else F32, (256, width), row)],
        [seq(d_own, *grad_own, *((corner, over, out_across) if fast else ())), d_other, w_qkv, w_qkv],
        flops=4 * SEQ * width * qkv_rows,
    )[0]
    if fast:
        whole = [one_part, swap_core(one_part)]
        part_b = seq(low_add(own_hi[:, mid:], over[1]), one_part)
        part_last = seq(low_add(far_lo[:, :mid], corner), one_part)
    else:
        whole = [sum_tp(one_part)]
    own_x, send_x, attn_part = call(
        partial(final_kernel, len(whole), 0, chunks),
        (SEQ // 256,),
        [((256, width), row), ((256, width), row), ((1, width), fixed)]
        + row_specs(whole, [], 256, width, SEQ),
        [
            ((SEQ, lane_width), F32, (256, lane_width), row),
            ((SEQ, lane_width), BF16, (256, lane_width), row),
            ((1, width), F32, (1, width), fixed),
        ],
        [seq(x_rows, part_b, part_last) if fast else x_rows, d_res, gain_one, *whole],
        table=out_table,
        scratch=[pltpu.VMEM((256, width), F32)],
    )
    input_grad = by_sequence(own_x, swap_dp(send_x).astype(F32))

    if fast:
        last = seq(own_f, attn_part)
        ffn_whole = [last, swap_core(last)]
        ffn_halves = [ffn_got, swap_core(ffn_got)]
    own_y, send_y = call(
        partial(output_kernel, len(ffn_whole), len(ffn_halves), chunks),
        (SEQ // 256,),
        [((256, width), row)] + row_specs(ffn_whole, ffn_halves, 256, width, SEQ),
        [((SEQ, lane_width), BF16, (256, lane_width), row)] * 2,
        [seq(residual, attn_part), *ffn_whole, *ffn_halves],
        table=out_table,
        scratch=[pltpu.VMEM((256, width), F32)],
    )
    got_y = swap_dp(send_y)
    layer_output = by_sequence(own_y, got_y)
    if fast:

        def sum_z(a):
            return jnp.sum(trade_z(a).astype(F32), axis=0)

        sum_ffn = lax.psum_scatter(grad_ffn, "tok", scatter_dimension=0, tiled=False)
        sum_ffn = seq(sum_ffn, own_y).astype(F32)

        sum_out = sum_z(low_add(out_lo, out_across))
        across_b, last = swap_x(part_b), swap_dp(part_last)
        across = jnp.concatenate([across_a, seq(across_b, own_y)], axis=1)
        near = jnp.concatenate([last, over[0]], axis=1)
        sum_qkv = sum_z((add(own_lo, across) + near.astype(F32)).astype(BF16))
    else:

        def stacked(g):
            return g.astype(F32).transpose(1, 0, 2).reshape(g.shape[1], -1)

        def wide_grad(g):
            even, odd = jnp.where(x == 0, g[0], g[1]), jnp.where(x == 0, g[1], g[0])
            return stacked(jnp.stack([even, odd], axis=1).reshape((-1,) + g[0].shape[1:]))

        sum_ffn = lax.psum_scatter(stacked(grad_ffn), "tok", scatter_dimension=1, tiled=True)

        def scatter_both(own, other):
            own = wide_grad(own) + swap_dp(wide_grad(other))
            return lax.psum_scatter(own, "tok", scatter_dimension=1, tiled=True)

        sum_out = scatter_both(grad_out_own, grad_out_other)
        sum_qkv = scatter_both(grad_own, grad_other)

    sum_gate, sum_up = sum_ffn[:hidden], sum_ffn[hidden : 2 * hidden]
    sum_down = sum_ffn[2 * hidden :]
    sum_qkv = sum_qkv.reshape(kv_rows, 512, -1)
    sum_query = sum_qkv[:, :256].reshape(kv_rows * 256, -1)
    sum_key = sum_qkv[:, 256:384].reshape(kv_rows * 128, -1)
    sum_value = sum_qkv[:, 384:].reshape(kv_rows * 128, -1)

    share = 1.0 / half
    gains = jnp.concatenate(
        [attn_part[0] * share, mlp_part[0] * share, gain_part[0], gain_part[1]]
    )
    if fast:
        gains = gains.reshape(-1, 128)
        for swap in (swap_core, swap_dp, swap_x):
            gains = gains + swap(gains)
        gains = seq(gains, got_y)
        for step in (1, 2):
            gains = gains + swap_z(step, gains)
        gains = gains.reshape(-1)
    else:
        gains = lax.psum(gains, ("tok", "col"))
    return (
        layer_output,
        input_grad,
        gains[:width],
        gains[width : 2 * width],
        gains[2 * width : 2 * width + 128],
        gains[2 * width + 128 :],
        sum_query,
        sum_key,
        sum_value,
        sum_out,
        sum_gate,
        sum_up,
        sum_down,
    )


def solution(mesh):
    rows, cols, both, every = P("tok"), P("col", "tok"), P("tok", "col"), P()
    in_specs = (both, both, rows, rows, every, every, every, every) + (cols,) * 7
    out_specs = (both, both, every, every, every, every) + (cols,) * 7
    return jax.shard_map(local, mesh=mesh, in_specs=in_specs, out_specs=out_specs, check_vma=False)
```

```python
import math
from functools import partial

import jax
import jax.numpy as jnp
from jax import lax
from jax.experimental import pallas as pl
from jax.experimental.pallas import tpu as pltpu
from jax.sharding import PartitionSpec as P

HEAD = 128
SEQ = 1024
NORM_EPS = 1e-06
ROPE_BASE = 1000000.0
NEG = -1e30
LOG2E = 1.4426950408889634
F32 = jnp.float32
BF16 = jnp.bfloat16
MIB = 1024 * 1024
HINT = 0.05


def dot_nt(a, b):
    return lax.dot_general(a, b, (((1,), (1,)), ((), ())), preferred_element_type=F32)


def dot_nn(a, b):
    return lax.dot_general(a, b, (((1,), (0,)), ((), ())), preferred_element_type=F32)


def dot_tn(a, b):
    return lax.dot_general(a, b, (((0,), (0,)), ((), ())), preferred_element_type=F32)


def seq(value, *after):
    return lax.optimization_barrier((value,) + after)[0]


def call(kernel, grid, ins, outs, args, table=None, scratch=(), flops=0, vmem=40):
    in_specs = [pl.BlockSpec(block, m) for block, m in ins]
    out_specs = [pl.BlockSpec(block, m) for _, _, block, m in outs]
    shapes = [jax.ShapeDtypeStruct(shape, dtype) for shape, dtype, _, _ in outs]
    nbytes = sum(a.size * a.dtype.itemsize for a in args)
    nbytes += sum(math.prod(s.shape) * s.dtype.itemsize for s in shapes)
    spec = pltpu.PrefetchScalarGridSpec(
        num_scalar_prefetch=0 if table is None else 1,
        grid=grid,
        in_specs=in_specs,
        out_specs=out_specs,
        scratch_shapes=list(scratch),
    )
    cost = pl.CostEstimate(flops=int(flops * HINT), bytes_accessed=int(nbytes * HINT), transcendentals=0)
    run = pl.pallas_call(
        kernel,
        out_shape=shapes,
        grid_spec=spec,
        cost_estimate=cost,
        compiler_params=pltpu.CompilerParams(vmem_limit_bytes=vmem * MIB),
    )
    return run(*args) if table is None else run(table, *args)


def assemble_kernel(slots, tab, a_ref, b_ref, o_ref):
    for p in range(slots):
        lanes = pl.ds(pl.multiple_of(tab[3 * p + 1] * 128, 128), 128)
        here = pl.ds(p * 128, 128)

        @pl.when(tab[3 * p + 2] == 0)
        def _():
            o_ref[:, here] = a_ref[tab[3 * p], :, lanes]

        @pl.when(tab[3 * p + 2] != 0)
        def _():
            o_ref[:, here] = b_ref[tab[3 * p], :, lanes]


def assemble_four_kernel(slots, tab, *refs):
    o_ref = refs[4]
    for p in range(slots):
        lanes = pl.ds(pl.multiple_of(tab[3 * p + 1] * 128, 128), 128)
        which = tab[3 * p] + 2 * tab[3 * p + 2]
        for i in range(4):

            @pl.when(which == i)
            def _(i=i, p=p, lanes=lanes):
                o_ref[:, pl.ds(p * 128, 128)] = refs[i][:, lanes]


def assemble_norm_kernel(slots, tab, a_ref, b_ref, gain_ref, x_ref, n_ref):
    assemble_kernel(slots, tab, a_ref, b_ref, x_ref)
    x = x_ref[...].astype(F32)
    r = lax.rsqrt(jnp.mean(x * x, axis=-1, keepdims=True) + NORM_EPS)
    n_ref[...] = (x * r * gain_ref[...]).astype(BF16)


def rope(u, cos, sin):
    return u * cos + pltpu.roll(u, HEAD // 2, axis=1) * sin


def rope_back(d, cos, sin):
    return d * cos - pltpu.roll(d, HEAD // 2, axis=1) * sin


def place(tab, w_ref, first, own_ref, across_ref):
    rows = pl.ds(first, own_ref.shape[1])
    for t in range(2 * own_ref.shape[0]):
        cols = pl.ds(t * 128, 128)

        @pl.when(tab[0] == t % 2)
        def _():
            w_ref[rows, cols] = own_ref[t // 2]

        @pl.when(tab[0] != t % 2)
        def _():
            w_ref[rows, cols] = across_ref[t // 2]


def project_kernel(groups, stacks, tab, n_ref, cos_ref, sin_ref, qg_ref, kg_ref, *refs):
    if stacks:
        o_ref, u_ref, r_ref, w_ref = refs[stacks:]

        @pl.when(pl.program_id(0) == 0)
        def _():
            near, across, far, corner_a, corner_b = refs[:stacks]
            rows = near.shape[1]
            mid = rows // 2
            place(tab, w_ref, 0, near, across)
            place(tab, w_ref, rows, far.at[:, 0:mid], corner_a)
            place(tab, w_ref, rows + mid, far.at[:, mid:rows], corner_b)
    else:
        w_ref, o_ref, u_ref, r_ref = refs
    n = n_ref[...]
    cos, sin = cos_ref[...], sin_ref[...]
    lane = lax.broadcasted_iota(jnp.int32, (n.shape[0], 128), 1)
    inverses = jnp.zeros((n.shape[0], 128), F32)
    for g in range(groups):
        out = dot_nt(n, w_ref[pl.ds(g * 512, 512), :])
        for i in range(3):
            u = out[:, i * 128 : (i + 1) * 128]
            r = lax.rsqrt(jnp.mean(u * u, axis=-1, keepdims=True) + NORM_EPS)
            u = u * r
            gain = qg_ref[...] if i < 2 else kg_ref[...]
            o_ref[:, pl.ds(g * 512 + i * 128, 128)] = rope(u * gain, cos, sin).astype(BF16)
            u_ref[:, pl.ds(g * 384 + i * 128, 128)] = u.astype(BF16)
            inverses = jnp.where(lane == g * 3 + i, r, inverses)
        o_ref[:, pl.ds(g * 512 + 384, 128)] = out[:, 384:].astype(BF16)
    r_ref[...] = inverses


def out_kernel(stacks, tab, m_ref, *refs):
    o_ref, w_ref = refs[2 * stacks :]

    @pl.when(pl.program_id(0) == 0)
    def _():
        for i in range(stacks):
            place(tab, w_ref, i * refs[2 * i].shape[1], refs[2 * i], refs[2 * i + 1])

    o_ref[...] = dot_nn(m_ref[...], w_ref[...]).astype(o_ref.dtype)


def visible(start_ref, first, rows, last):
    start = start_ref[:, pl.ds(first, rows)]
    start = jnp.concatenate([start, start], axis=1)
    key = lax.broadcasted_iota(jnp.int32, (last, 2 * rows), 0)
    query = lax.broadcasted_iota(jnp.int32, (1, 2 * rows), 1)
    query = jnp.where(query >= rows, query - rows, query) + first
    return (key >= start) & (key <= query)


def attend_kernel(rows, qkv_ref, start_ref, o_ref, l_ref):
    scale = HEAD**-0.5 * LOG2E
    for i in range(SEQ // rows):
        first, last = i * rows, (i + 1) * rows
        span = pl.ds(first, rows)
        q = jnp.concatenate([qkv_ref[span, 0:128], qkv_ref[span, 128:256]], axis=0)
        s = dot_nt(qkv_ref[0:last, 256:384], q) * scale
        s = jnp.where(visible(start_ref, first, rows, last), s, NEG)
        m = jnp.max(s, axis=0, keepdims=True)
        e = jnp.exp2(s - m)
        total = jnp.sum(e, axis=0, keepdims=True)
        o = dot_tn(qkv_ref[0:last, 384:512], e.astype(BF16)) * (1.0 / total)
        o = o.T.astype(BF16)
        o_ref[span, 0:128] = o[:rows]
        o_ref[span, 128:256] = o[rows:]
        log_total = m + jnp.log2(total)
        l_ref[0, 0:1, span] = log_total[:, :rows]
        l_ref[0, 1:2, span] = log_total[:, rows:]


def attend_back_kernel(
    rows, base, qkv_ref, do_ref, l_ref, start_ref, u_ref, r_ref, cos_ref, sin_ref, qg_ref, kg_ref,
    o_ref, gain_ref, dk_ref, dv_ref,
):
    g = pl.program_id(0) + base
    scale = HEAD**-0.5

    @pl.when(pl.program_id(0) == 0)
    def _():
        gain_ref[...] = jnp.zeros_like(gain_ref)

    lane = lax.broadcasted_iota(jnp.int32, (SEQ, 128), 1)

    def through(grad, head, span, gain):
        u = u_ref[span, pl.ds(head * 128, 128)].astype(F32)
        picked = jnp.where(lane[: grad.shape[0]] == g * 3 + head, r_ref[span, :], 0.0)
        r = jnp.sum(picked, axis=-1, keepdims=True)
        d = rope_back(grad, cos_ref[span, :], sin_ref[span, :])
        gain_part = jnp.sum(d * u, axis=0, keepdims=True)
        d = d * gain
        d = r * (d - u * jnp.mean(u * d, axis=-1, keepdims=True))
        return d.astype(BF16), gain_part

    q_part = jnp.zeros((1, HEAD), F32)
    for i in reversed(range(SEQ // rows)):
        first, last = i * rows, (i + 1) * rows
        span = pl.ds(first, rows)
        keys = pl.ds(0, last)
        q = jnp.concatenate([qkv_ref[span, 0:128], qkv_ref[span, 128:256]], axis=0)
        do = jnp.concatenate([do_ref[span, 0:128], do_ref[span, 128:256]], axis=0)
        log_total = jnp.concatenate([l_ref[0, 0:1, span], l_ref[0, 1:2, span]], axis=1)
        k = qkv_ref[0:last, 256:384]
        s = dot_nt(k, q) * (scale * LOG2E)
        s = jnp.where(visible(start_ref, first, rows, last), s, NEG)
        p = jnp.exp2(s - log_total)
        t = p * dot_nt(qkv_ref[0:last, 384:512], do)
        ds = (t - p * jnp.sum(t, axis=0, keepdims=True)).astype(BF16)
        dv = dot_nn(p.astype(BF16), do)
        dk = dot_nn(ds, q)
        if last == SEQ:
            dv_ref[...] = dv
            dk_ref[...] = dk
        else:
            dv_ref[keys, :] += dv
            dk_ref[keys, :] += dk
        dq = (dot_tn(k, ds) * scale).T
        for head in range(2):
            out, part = through(dq[head * rows : (head + 1) * rows], head, span, qg_ref[...])
            o_ref[span, pl.ds(head * 128, 128)] = out
            q_part += part
    out, k_part = through(dk_ref[...] * scale, 2, pl.ds(0, SEQ), kg_ref[...])
    o_ref[:, 256:384] = out
    o_ref[:, 384:512] = dv_ref[...].astype(BF16)
    gain_ref[0:1, :] += q_part
    gain_ref[1:2, :] += k_part


def residual_kernel(parts, x_ref, *refs):
    total = x_ref[...].astype(F32)
    for ref in refs[:parts]:
        total += ref[...].astype(F32)
    gain_ref, res_ref, n_ref = refs[parts:]
    r = lax.rsqrt(jnp.mean(total * total, axis=-1, keepdims=True) + NORM_EPS)
    res_ref[...] = total
    n_ref[...] = (total * r * gain_ref[...]).astype(BF16)


def ffn_join_kernel(tab, n_ref, c_ref, g_ref, near_ref, across_ref, h_ref, f_ref, t_ref, w_ref):
    count = w_ref.shape[0] // 3

    @pl.when(pl.program_id(0) == 0)
    def _():
        for t in range(g_ref.shape[0]):
            w_ref[0:count, t * 128 : (t + 1) * 128] = g_ref[t]
        place(tab, w_ref, count, near_ref, across_ref)

    parts = [w_ref.at[pl.ds(i * count, count), :] for i in range(3)]
    ffn_kernel(n_ref, c_ref, *parts, h_ref, f_ref, t_ref)


def ffn_kernel(n_ref, c_ref, wg_ref, wu_ref, wd_ref, h_ref, f_ref, t_ref):
    n = n_ref[...]
    width = wg_ref.shape[0]
    gate = dot_nt(n, wg_ref[...])
    up = dot_nt(n, wu_ref[...])
    dh = dot_nt(c_ref[...], wd_ref[...])
    sig = 1.0 / (1.0 + jnp.exp2(gate * -LOG2E))
    act = gate * sig
    hidden = (act * up).astype(BF16)
    du = (dh * act).astype(BF16)
    dg = (dh * up * sig * (1.0 + gate * (1.0 - sig))).astype(BF16)
    h_ref[:, 0:width] = dg
    h_ref[:, width : 2 * width] = du
    h_ref[:, 2 * width :] = hidden
    f_ref[...] = dot_nn(hidden, wd_ref[...]).astype(BF16)
    t_ref[...] = (dot_nn(dg, wg_ref[...]) + dot_nn(du, wu_ref[...])).astype(BF16)


def sum_parts(whole, halves, tab):
    total = None
    for ref in whole:
        part = ref[...].astype(F32)
        total = part if total is None else total + part
    if halves:
        per = pl.num_programs(0) // 2
        mine = pl.program_id(0) // per != tab[0]
        total += jnp.where(mine, halves[0][...].astype(F32), halves[1][...].astype(F32))
    return total


def pick_blocks(count, tab, base, source, own_ref, send_ref):
    for which, ref in enumerate((own_ref, send_ref)):
        for i in range(count):
            at = tab[base + which * count + i]
            lanes = pl.ds(pl.multiple_of(at * 128, 128), 128)
            ref[:, i * 128 : (i + 1) * 128] = source[:, lanes].astype(ref.dtype)


def middle_kernel(whole, half, tab, res_ref, cot_ref, gain_ref, *refs):
    two = sum_parts(refs[:whole], refs[whole : whole + half], tab)
    dres_ref, low_ref, part_ref = refs[whole + half :]
    res = res_ref[...]
    width = res.shape[-1]
    r = lax.rsqrt(jnp.mean(res * res, axis=-1, keepdims=True) + NORM_EPS)
    scaled = two * gain_ref[...]
    inner = jnp.sum(scaled * res, axis=-1, keepdims=True)
    grad = cot_ref[...].astype(F32) + r * scaled - res * (r * r * r * (inner / width))
    dres_ref[...] = grad
    low_ref[...] = grad.astype(BF16)

    @pl.when(pl.program_id(0) == 0)
    def _():
        part_ref[...] = jnp.zeros_like(part_ref)

    part_ref[...] += jnp.sum(two * res * r, axis=0, keepdims=True)


def output_kernel(whole, half, count, tab, res_ref, *refs):
    total = sum_parts(refs[:whole], refs[whole : whole + half], tab)
    own_ref, send_ref, hold = refs[whole + half :]
    hold[...] = res_ref[...] + total
    pick_blocks(count, tab, 1, hold, own_ref, send_ref)


def final_kernel(whole, half, count, tab, x_ref, dres_ref, gain_ref, *refs):
    one = sum_parts(refs[:whole], refs[whole : whole + half], tab)
    own_ref, send_ref, part_ref, hold = refs[whole + half :]
    x = x_ref[...].astype(F32)
    width = x.shape[-1]
    r = lax.rsqrt(jnp.mean(x * x, axis=-1, keepdims=True) + NORM_EPS)
    scaled = one * gain_ref[...]
    inner = jnp.sum(scaled * x, axis=-1, keepdims=True)
    hold[...] = dres_ref[...] + r * scaled - x * (r * r * r * (inner / width))
    pick_blocks(count, tab, 1, hold, own_ref, send_ref)

    @pl.when(pl.program_id(0) == 0)
    def _():
        part_ref[...] = jnp.zeros_like(part_ref)

    part_ref[...] += jnp.sum(one * x * r, axis=0, keepdims=True)


def two_dots_kernel(a_ref, b_ref, v_ref, w_ref, o_ref):
    o_ref[...] = (dot_nn(a_ref[...], v_ref[...]) + dot_nn(b_ref[...], w_ref[...])).astype(o_ref.dtype)


def grad_kernel(tab, a_ref, b_ref, lo_ref, hi_ref):
    total = dot_tn(a_ref[...], b_ref[...]).astype(BF16)
    for t in range(2 * lo_ref.shape[0]):
        part = total[:, t * 128 : (t + 1) * 128]

        @pl.when(tab[0] == t % 2)
        def _():
            lo_ref[t // 2] = part

        @pl.when(tab[0] != t % 2)
        def _():
            hi_ref[t // 2] = part


def ffn_grad_kernel(spans, switch, *refs):
    rows, (cot_ref, o_ref) = refs[: 2 * spans], refs[2 * spans :]

    def put(total):
        total = total.astype(BF16)
        for t in range(o_ref.shape[0]):
            o_ref[t] = total[:, t * 128 : (t + 1) * 128]

    @pl.when(pl.program_id(0) < switch)
    def _():
        put(sum(dot_tn(rows[2 * i][...], rows[2 * i + 1][...]) for i in range(spans)))

    @pl.when(pl.program_id(0) >= switch)
    def _():
        first, total = 0, None
        for i in range(spans):
            count = rows[2 * i].shape[0]
            part = dot_tn(rows[2 * i][...], cot_ref[first : first + count, :])
            total = part if total is None else total + part
            first += count
        put(total)


def weight_grad(a, b, first, count, side, block=256):
    rows, width = b.shape
    block = min(block, count)
    base = first // block
    half = width // 256
    stack = ((half, count, 128), BF16, (half, block, 128), lambda i, *_: (0, i, 0))
    return call(
        grad_kernel,
        (count // block,),
        [((rows, block), lambda i, *_: (0, base + i)), ((rows, width), lambda i, *_: (0, 0))],
        [stack, stack],
        [a, b],
        table=side,
        flops=2 * rows * count * width,
    )


def ffn_grads(spans, cot, block=256):
    width = cot.shape[1]
    inner = spans[0][0].shape[1]
    block = math.gcd(block, inner // 3)
    ins, args = [], []
    for h, n in spans:
        ins += [((h.shape[0], block), lambda i: (0, i)), (n.shape, lambda i: (0, 0))]
        args += [h, n]
    pieces = width // 128
    return call(
        partial(ffn_grad_kernel, len(spans), 2 * inner // 3 // block),
        (inner // block,),
        ins + [(cot.shape, lambda i: (0, 0))],
        [((pieces, inner, 128), BF16, (pieces, block, 128), lambda i: (0, i, 0))],
        args + [cot],
        flops=2 * cot.shape[0] * inner * width,
        vmem=48,
    )[0]


def ffn(n, rows, cot, cot_first, w, side=None, block=256):
    width = n.shape[1]
    hidden = w[0].shape[1] if side is not None else w.shape[0] // 3
    base = cot_first // block
    outer = ((rows, width), BF16, (block, width), lambda i, *_: (i, 0))
    outs = [((rows, 3 * hidden), BF16, (block, 3 * hidden), lambda i, *_: (i, 0)), outer, outer]
    ins = [((block, width), lambda i, *_: (i, 0)), ((block, width), lambda i, *_: (base + i, 0))]
    if side is not None:
        ins += [(a.shape, lambda i, *_, k=a.ndim: (0,) * k) for a in w]
        outs += [((3 * hidden, width), BF16, (3 * hidden, width), lambda i, *_: (0, 0))]
    else:
        ins += [((hidden, width), lambda i, k=k: (k, 0)) for k in range(3)]
    return call(
        ffn_kernel if side is None else ffn_join_kernel,
        (rows // block,),
        ins,
        outs,
        [n, cot] + ([w, w, w] if side is None else w),
        table=side,
        flops=12 * rows * width * hidden,
        vmem=48,
    )


def row_specs(parts, halves, block, width, rows):
    per = rows // block // 2
    ins = [((block, width), lambda i, *_: (i, 0)) for _ in parts]
    ins += [((block, width), lambda i, *_: (i % per, 0)) for _ in halves]
    return ins


def local(
    layer_input, cotangent, doc_ids, positions, attn_gain, mlp_gain, query_gain, key_norm_gain,
    query_weight, key_matrix, value_matrix, output_weight, gate_weight, up_weight, down_weight,
):
    rows, lane_width = layer_input.shape
    nt, nc = lax.axis_size("tok"), lax.axis_size("col")
    width = lane_width * nc
    half = nc // 2
    tok, col = lax.axis_index("tok"), lax.axis_index("col")
    dp, tp = col // half, col % half
    fast = nt == 8 and nc == 4 and width // nt == 128
    chunks = lane_width // 128

    def swap_dp(a):
        return lax.ppermute(a, "col", [(j, (j + half) % nc) for j in range(nc)])

    def swap_core(a):
        return lax.ppermute(a, "col", [(j, j ^ 1) for j in range(nc)])

    groups = [[d * half + t for t in range(half)] for d in range(2)]

    def sum_tp(a):
        return lax.psum(a.astype(F32), "col", axis_index_groups=groups)

    def swap_x(a):
        return lax.ppermute(a, "tok", [(t, t ^ 1) for t in range(nt)])

    def swap_z(step, a):
        return lax.ppermute(a, "tok", [(t, (t // 2 ^ step) * 2 + t % 2) for t in range(nt)])

    lines = [[z * 2 + x for z in range(nt // 2)] for x in range(2)]

    def share_z(a):
        copies = jnp.broadcast_to(a[None], (nt // 2,) + a.shape)
        return lax.all_to_all(copies, "tok", 0, 0, axis_index_groups=lines)

    def trade_z(a):
        return lax.all_to_all(a, "tok", 0, 0, axis_index_groups=lines)

    x = tok % 2
    side = x[None].astype(jnp.int32)
    pieces = width // 128

    out_table = [tp]
    for block in (col, (col + half) % nc):
        out_table += [block * chunks + i for i in range(chunks)]
    out_table = jnp.stack([jnp.asarray(t, jnp.int32) for t in out_table])

    kv_rows = key_matrix.shape[0] // HEAD
    mixed_weight = []
    for g in range(kv_rows):
        mixed_weight += [
            query_weight[g * 256 : (g + 1) * 256],
            key_matrix[g * 128 : (g + 1) * 128],
            value_matrix[g * 128 : (g + 1) * 128],
        ]
    own_qkv = jnp.concatenate(mixed_weight, axis=0).astype(BF16)
    own_out = output_weight.astype(BF16)
    own_ffn = jnp.concatenate([gate_weight, up_weight, down_weight], axis=0).astype(BF16)
    hidden = gate_weight.shape[0]

    if not fast:

        def gather(p):
            return lax.all_gather(p, "tok", axis=1, tiled=True)

        def gather_both(p):
            own = gather(p)
            return jnp.concatenate([own, swap_dp(own)], axis=0)

    place = lax.dynamic_slice_in_dim(positions, dp * SEQ, SEQ).astype(F32)
    steps = jnp.arange(HEAD // 2, dtype=F32)
    frequency = jnp.exp(steps * (-2.0 * math.log(ROPE_BASE) / HEAD))
    angle = place[:, None] * frequency[None, :]
    cosine, sine = jnp.cos(angle), jnp.sin(angle)
    cosine = jnp.concatenate([cosine, cosine], axis=1)
    sine = jnp.concatenate([-sine, sine], axis=1)
    docs = lax.dynamic_slice_in_dim(doc_ids, dp * SEQ, SEQ)
    start = jnp.sum((docs[:, None] < docs[None, :]).astype(jnp.int32), axis=0)[None, :]
    query_row, key_row = query_gain[None, :], key_norm_gain[None, :]

    gain_one, gain_two = attn_gain[None, :], mlp_gain[None, :]

    def seq_rows(a, which):
        return lax.dynamic_slice_in_dim(a, which * SEQ, SEQ, axis=0)

    if fast:
        in_table = []
        for t in range(pieces):
            block = t // chunks
            in_table += [
                (block // half != dp).astype(jnp.int32),
                jnp.int32(t % chunks),
                (block % half != tp).astype(jnp.int32),
            ]
        in_table = jnp.stack(in_table)
        got = swap_dp(seq_rows(layer_input, 1 - dp))
        mine = jnp.stack([seq_rows(layer_input, dp), got])
        other = swap_core(mine)

        spec = ((2, 256, lane_width), lambda i, *_: (0, i, 0))
        row = ((SEQ, width), BF16, (256, width), lambda i, *_: (i, 0))
        x_rows, normed_one = call(
            partial(assemble_norm_kernel, pieces),
            (SEQ // 256,),
            [spec, spec, ((1, width), lambda i, *_: (0, 0))],
            [row, row],
            [mine, other, gain_one],
            table=in_table,
        )
        mid = own_qkv.shape[0] // 2
        gate_all = lax.all_gather(own_ffn[:hidden], "tok")
        qkv_z = seq(share_z(own_qkv), normed_one, cosine, sine, start)
        out_z = share_z(seq(own_out, qkv_z))
        qkv_x, qkv_y = swap_x(qkv_z), swap_dp(qkv_z)
        corner_x = swap_x(seq(qkv_y[:, :mid], out_z))
        corner_y = swap_dp(seq(qkv_x[:, mid:], out_z))
        qkv_stacks = [qkv_z, qkv_x, qkv_y, corner_x, corner_y]
        late_z = share_z(seq(own_ffn[hidden:], out_z))
        out_z = seq(out_z, corner_x, corner_y)
        out_x, out_y = swap_x(out_z), swap_dp(out_z)
        cot_sib = swap_core(cotangent)

        def cot_map(i, tab):
            d, t = tab[24], tab[25]
            return (jnp.where(i < 2, d * 2 + i, (1 - d) * 2 + (i - 2 + t) % 2), 0)

    else:
        w_qkv, w_out = gather_both(own_qkv), gather_both(own_out)
        w_ffn = gather(own_ffn)
        whole_input = lax.all_gather(layer_input, "col", axis=1, tiled=True)
        whole_cot = lax.all_gather(cotangent, "col", axis=1, tiled=True)
        x_rows = seq_rows(whole_input, dp)
        cot_rows = jnp.concatenate([seq_rows(whole_cot, dp), seq_rows(whole_cot, 1 - dp)], axis=0)
        wide = x_rows.astype(F32)
        inverse = lax.rsqrt(jnp.mean(wide * wide, axis=-1, keepdims=True) + NORM_EPS)
        normed_one = (wide * inverse * gain_one).astype(BF16)

    count = 2 * kv_rows
    row = lambda i, *_: (i, 0)
    fixed = lambda i, *_: (0, 0)
    by_head = lambda i, *_: (0, i)
    stack_spec = lambda a: (a.shape, lambda i, *_: (0, 0, 0))
    ins = [
        ((256, width), row),
        ((256, 128), row),
        ((256, 128), row),
        ((1, 128), fixed),
        ((1, 128), fixed),
    ]
    outs = [
        ((SEQ, count * 512), BF16, (256, count * 512), row),
        ((SEQ, count * 384), BF16, (256, count * 384), row),
        ((SEQ, 128), F32, (256, 128), row),
    ]
    args = [normed_one, cosine, sine, query_row, key_row]
    whole_w = ((count * 512, width), fixed)
    project_flops = 2 * SEQ * width * count * 512
    if fast:
        qkv, unit, inverses, w_qkv = call(
            partial(project_kernel, count, len(qkv_stacks)),
            (SEQ // 256,),
            ins + [stack_spec(a) for a in qkv_stacks],
            outs + [((count * 512, width), BF16, *whole_w)],
            args + qkv_stacks,
            table=side,
            flops=project_flops,
        )
    else:
        qkv, unit, inverses = call(
            partial(project_kernel, count, 0),
            (SEQ // 256,),
            ins + [whole_w],
            outs,
            args + [w_qkv],
            table=side,
            flops=project_flops,
        )
    if fast:
        out_xy = swap_dp(seq(out_x, out_y, unit))
        cot_got = swap_dp(seq(cotangent, out_xy))
        cot_sib_got = swap_core(cot_got)
        out_stacks = [out_z, out_x, out_y, out_xy]
        late_x = swap_x(seq(late_z, out_x))
        ffn_stacks = [gate_all, late_z, late_x]
    head_block = lambda n: ((SEQ, n), by_head)
    log_block = ((1, 2, SEQ), lambda i, *_: (i, 0, 0))
    mixed, log_total = call(
        partial(attend_kernel, 256),
        (count,),
        [head_block(512), ((1, SEQ), fixed)],
        [
            ((SEQ, count * 256), BF16, (SEQ, 256), by_head),
            ((count, 2, SEQ), F32, (1, 2, SEQ), lambda i, *_: (i, 0, 0)),
        ],
        [seq(qkv, out_x, out_y, late_z) if fast else qkv, start],
        flops=8 * SEQ * SEQ * HEAD * count,
    )
    if fast:
        heads_width = count * 256
        out_part, w_out = call(
            partial(out_kernel, len(out_stacks) // 2),
            (SEQ // 256,),
            [((256, heads_width), row)] + [stack_spec(a) for a in out_stacks],
            [
                ((SEQ, width), BF16, (256, width), row),
                ((heads_width, width), BF16, (heads_width, width), fixed),
            ],
            [mixed, *out_stacks],
            table=side,
            flops=2 * SEQ * heads_width * width,
        )
        parts = [out_part, swap_core(out_part)]
    else:
        parts = [sum_tp(dot_nn(mixed, w_out))]
    residual, normed_two = call(
        partial(residual_kernel, len(parts)),
        (SEQ // 256,),
        [((256, width), row)] * (1 + len(parts)) + [((1, width), fixed)],
        [
            ((SEQ, width), F32, (256, width), row),
            ((SEQ, width), BF16, (256, width), row),
        ],
        [seq(x_rows, cot_sib_got) if fast else x_rows, *parts, gain_two],
    )

    if fast:
        mid = SEQ // 2
        piece = lax.dynamic_slice_in_dim(normed_two, tp * mid, mid, axis=0)
        near = swap_dp(piece)
        far = swap_core(near)
        spec = ((512, lane_width), cot_map)
        cot_rows = call(
            partial(assemble_four_kernel, pieces),
            (4,),
            [spec] * 4,
            [((2 * SEQ, width), BF16, (512, width), lambda i, *_: (i, 0))],
            [seq(cotangent, normed_two), cot_got, cot_sib, cot_sib_got],
            table=jnp.concatenate([in_table, jnp.stack([dp, tp]).astype(jnp.int32)]),
        )[0]
        near_h, near_f, near_t, w_ffn = ffn(near, mid, cot_rows, SEQ, ffn_stacks, side)
        far_h, far_f, far_t = ffn(seq(far, near_t), mid, cot_rows, SEQ + mid, w_ffn)
        two_mine = (far_t.astype(F32) + swap_core(near_t).astype(F32)).astype(BF16)
        two_got = swap_dp(two_mine)
        own_h, own_f, own_t = ffn(seq(normed_two, two_mine), SEQ, cot_rows, 0, w_ffn)
        own_sib = swap_core(own_t)
        ffn_mine = (seq(far_f, own_t).astype(F32) + swap_core(near_f).astype(F32)).astype(BF16)
        grad_ffn = ffn_grads(
            [(own_h, normed_two), (near_h, near), (far_h, far)], seq(cot_rows, ffn_mine)
        )
        two_sib = swap_core(seq(two_got, grad_ffn))
        grad_ffn = seq(grad_ffn, two_got)
        whole, halves = [own_t, own_sib], [two_got, two_sib]
    else:
        normed_other = swap_dp(normed_two)
        own_h, own_f, own_t = ffn(normed_two, SEQ, cot_rows, 0, w_ffn)
        other_h, other_f, other_t = ffn(normed_other, SEQ, cot_rows, SEQ, w_ffn)
        grad_ffn = ffn_grads([(own_h, normed_two), (other_h, normed_other)], cot_rows)
        whole = [sum_tp(own_t) + swap_dp(sum_tp(other_t))]
        ffn_whole = [sum_tp(own_f) + swap_dp(sum_tp(other_f))]
        halves, ffn_halves = [], []

    d_res, d_low, mlp_part = call(
        partial(middle_kernel, len(whole), len(halves)),
        (SEQ // 256,),
        [((256, width), row), ((256, width), row), ((1, width), fixed)]
        + row_specs(whole, halves, 256, width, SEQ),
        [
            ((SEQ, width), F32, (256, width), row),
            ((SEQ, width), BF16, (256, width), row),
            ((1, width), F32, (1, width), fixed),
        ],
        [residual, cot_rows, gain_two, *whole, *halves],
        table=out_table,
    )

    def by_sequence(own, other):
        return jnp.where(
            dp == 0,
            jnp.concatenate([own, other], axis=0),
            jnp.concatenate([other, own], axis=0),
        )

    def add(a, b):
        return a.astype(F32) + b.astype(F32)

    def low_add(a, b):
        return add(a, b).astype(BF16)

    d_mixed = dot_nt(d_low, w_out).astype(BF16)
    out_rows = mixed.shape[1] // 2
    grad_out_other = weight_grad(mixed, d_low, out_rows, out_rows, side)
    grad_out_own = weight_grad(mixed, d_low, 0, out_rows, side)

    def attend_back(base, some, after):
        cols = lambda n: ((SEQ, n), lambda i, *_: (0, base + i))
        return call(
            partial(attend_back_kernel, 256, base),
            (some,),
            [
                cols(512),
                cols(256),
                ((1, 2, SEQ), lambda i, *_: (base + i, 0, 0)),
                ((1, SEQ), fixed),
                cols(384),
                ((SEQ, 128), fixed),
                ((SEQ, 128), fixed),
                ((SEQ, 128), fixed),
                ((1, 128), fixed),
                ((1, 128), fixed),
            ],
            [
                ((SEQ, some * 512), BF16, (SEQ, 512), by_head),
                ((8, 128), F32, (8, 128), fixed),
            ],
            [
                qkv, seq(d_mixed, *after), log_total, start, unit, inverses, cosine, sine,
                query_row, key_row,
            ],
            scratch=[pltpu.VMEM((SEQ, 128), F32), pltpu.VMEM((SEQ, 128), F32)],
            flops=20 * SEQ * SEQ * HEAD * some,
        )

    some = count // 2
    qkv_rows = some * 512
    d_other, gains_other = attend_back(some, some, (*grad_out_other, *grad_out_own))
    grad_other = weight_grad(d_other, normed_one, 0, qkv_rows, side)
    if fast:
        out_over = swap_dp(jnp.stack(grad_out_other))
        far_lo, far_hi = grad_other
        mid = qkv_rows // 2
        corner = swap_x(far_hi[:, :mid])
        over = swap_dp(seq(jnp.stack([far_lo[:, mid:], far_hi[:, mid:]]), out_over))
        ffn_got = swap_dp(seq(ffn_mine, over))
    d_own, gains_own = attend_back(0, some, grad_other)
    gain_part = gains_own + gains_other
    grad_own = weight_grad(
        seq(d_own, out_over) if fast else d_own, normed_one, 0, qkv_rows, side
    )
    if fast:
        own_lo, own_hi = grad_own
        out_lo = low_add(grad_out_own[0], out_over[0])
        out_hi = low_add(grad_out_own[1], out_over[1])
        out_across = swap_x(out_hi)
    wide = ((256, qkv_rows), row)
    one_part = call(
        two_dots_kernel,
        (SEQ // 256,),
        [
            wide,
            wide,
            ((qkv_rows, width), lambda i: (0, 0)),
            ((qkv_rows, width), lambda i: (1, 0)),
        ],
        [((SEQ, width), BF16 if fast else F32, (256, width), row)],
        [seq(d_own, *grad_own, *((corner, over) if fast else ())), d_other, w_qkv, w_qkv],
        flops=4 * SEQ * width * qkv_rows,
    )[0]
    if fast:
        whole = [one_part, swap_core(one_part)]
        part_b = low_add(seq(own_hi, one_part)[:, mid:], over[1])
        part_b = jnp.concatenate([own_hi[:, :mid], part_b], axis=1)
        part_last = seq(low_add(far_lo[:, :mid], corner), one_part)
    else:
        whole = [sum_tp(one_part)]
    own_x, send_x, attn_part = call(
        partial(final_kernel, len(whole), 0, chunks),
        (SEQ // 256,),
        [((256, width), row), ((256, width), row), ((1, width), fixed)]
        + row_specs(whole, [], 256, width, SEQ),
        [
            ((SEQ, lane_width), F32, (256, lane_width), row),
            ((SEQ, lane_width), BF16, (256, lane_width), row),
            ((1, width), F32, (1, width), fixed),
        ],
        [seq(x_rows, part_b, part_last, out_across) if fast else x_rows, d_res, gain_one, *whole],
        table=out_table,
        scratch=[pltpu.VMEM((256, width), F32)],
    )
    input_grad = by_sequence(own_x, swap_dp(send_x).astype(F32))

    if fast:
        last = seq(own_f, attn_part)
        ffn_whole = [last, swap_core(last)]
        ffn_halves = [ffn_got, swap_core(ffn_got)]
    own_y, send_y = call(
        partial(output_kernel, len(ffn_whole), len(ffn_halves), chunks),
        (SEQ // 256,),
        [((256, width), row)] + row_specs(ffn_whole, ffn_halves, 256, width, SEQ),
        [((SEQ, lane_width), BF16, (256, lane_width), row)] * 2,
        [seq(residual, attn_part), *ffn_whole, *ffn_halves],
        table=out_table,
        scratch=[pltpu.VMEM((256, width), F32)],
    )
    got_y = swap_dp(send_y)
    layer_output = by_sequence(own_y, got_y)
    if fast:

        def sum_z(a):
            return jnp.sum(trade_z(a).astype(F32), axis=0)

        sum_ffn = lax.psum_scatter(grad_ffn, "tok", scatter_dimension=0, tiled=False)
        sum_ffn = seq(sum_ffn, own_y).astype(F32)

        sum_out = sum_z(low_add(out_lo, out_across))
        across, last = swap_x(part_b), swap_dp(part_last)
        across = seq(across, own_y)
        near = jnp.concatenate([last, over[0]], axis=1)
        traded = trade_z((add(own_lo, across) + near.astype(F32)).astype(BF16))
        sum_ffn = [sum_ffn[i * hidden : (i + 1) * hidden] for i in range(3)]
        traded = seq(traded, sum_out, *sum_ffn)
        traded = traded.reshape(-1, kv_rows, 512, 128)
        sum_query, sum_key, sum_value = [
            jnp.sum(traded[:, :, a:b].astype(F32), axis=0).reshape(kv_rows * (b - a), 128)
            for a, b in ((0, 256), (256, 384), (384, 512))
        ]
    else:

        def stacked(g):
            return g.astype(F32).transpose(1, 0, 2).reshape(g.shape[1], -1)

        def wide_grad(g):
            even, odd = jnp.where(x == 0, g[0], g[1]), jnp.where(x == 0, g[1], g[0])
            return stacked(jnp.stack([even, odd], axis=1).reshape((-1,) + g[0].shape[1:]))

        sum_ffn = lax.psum_scatter(stacked(grad_ffn), "tok", scatter_dimension=1, tiled=True)

        def scatter_both(own, other):
            own = wide_grad(own) + swap_dp(wide_grad(other))
            return lax.psum_scatter(own, "tok", scatter_dimension=1, tiled=True)

        sum_out = scatter_both(grad_out_own, grad_out_other)
        sum_qkv = scatter_both(grad_own, grad_other).reshape(kv_rows, 512, -1)
        sum_query, sum_key, sum_value = [
            sum_qkv[:, a:b].reshape(kv_rows * (b - a), -1)
            for a, b in ((0, 256), (256, 384), (384, 512))
        ]
        sum_ffn = [sum_ffn[i * hidden : (i + 1) * hidden] for i in range(3)]

    share = 1.0 / half
    gains = jnp.concatenate(
        [attn_part[0] * share, mlp_part[0] * share, gain_part[0], gain_part[1]]
    )
    if fast:
        gains = gains.reshape(-1, 128)
        for swap in (swap_core, swap_dp, swap_x):
            gains = gains + swap(gains)
        gains = seq(gains, got_y)
        for step in (1, 2):
            gains = gains + swap_z(step, gains)
        gains = gains.reshape(-1)
    else:
        gains = lax.psum(gains, ("tok", "col"))
    return (
        layer_output,
        input_grad,
        gains[:width],
        gains[width : 2 * width],
        gains[2 * width : 2 * width + 128],
        gains[2 * width + 128 :],
        sum_query,
        sum_key,
        sum_value,
        sum_out,
        sum_ffn[0],
        sum_ffn[1],
        sum_ffn[2],
    )


def solution(mesh):
    rows, cols, both, every = P("tok"), P("col", "tok"), P("tok", "col"), P()
    in_specs = (both, both, rows, rows, every, every, every, every) + (cols,) * 7
    out_specs = (both, both, every, every, every, every) + (cols,) * 7
    return jax.shard_map(local, mesh=mesh, in_specs=in_specs, out_specs=out_specs, check_vma=False)
```
